32 devices in a mesh: dp: 8 (over z, y), tensor: 4 (over x, core).
Axes of the slice: x: 2, y: 2, z: 4, core: 2. Of those that a mesh axis runs over, the one named last changes fastest.
Arguments:
- block_input: bfloat16 [4096, 2048], P(('dp', 'tensor')), may hold values from -6 to 6
- cotangent: bfloat16 [4096, 2048], P(('dp', 'tensor')), may hold values from -6 to 6
- sequence_blocks: int32 [2], replicated, may hold values from 4 to 12, as said below
- gain_attention: float32 [2048], replicated, may hold values from 0.5 to 1.5
- query_weight: bfloat16 [2048, 2048], P(None, 'tensor'), may hold values from -0.125 to 0.125
- keyval_weight: bfloat16 [2048, 256], replicated, may hold values from -0.125 to 0.125
- output_weight: bfloat16 [2048, 2048], P(None, 'tensor'), may hold values from -2 to 2
- gain_feedforward: float32 [2048], replicated, may hold values from 0.5 to 1.5
- gate_weight: bfloat16 [2048, 6144], P(None, 'tensor'), may hold values from -0.125 to 0.125
- up_weight: bfloat16 [2048, 6144], P(None, 'tensor'), may hold values from -0.125 to 0.125
- down_weight: bfloat16 [2048, 6144], P(None, 'tensor'), may hold values from -0.078125 to 0.078125
Outputs:
- block_output: bfloat16 [4096, 2048], P(('dp', 'tensor'))
- grad_input: float32 [4096, 2048], P(('dp', 'tensor'))
- grad_gain_attention: float32 [2048], P('dp')
- grad_query: float32 [2048, 2048], P('dp', 'tensor')
- grad_keyval: float32 [2048, 256], P('dp')
- grad_output_weight: float32 [2048, 2048], P('dp', 'tensor')
- grad_gain_feedforward: float32 [2048], P('dp')
- grad_gate: float32 [2048, 6144], P('dp', 'tensor')
- grad_up: float32 [2048, 6144], P('dp', 'tensor')
- grad_down: float32 [2048, 6144], P('dp', 'tensor')
The draws below stay inside these ranges and needn't reach their ends.
Inputs may be any that keep to these rules, and one draw needn't show every extreme that they name: Sequence n is sequence_blocks[n] whole blocks of 256 tokens; the 2 lengths add up to 16, and one of them is exactly 12.
All inputs are finite; a program needn't handle non-finite values.
Results may differ from the reference program's by a relative error of at most 0.014.
Values may be sent and summed in bfloat16 or wider, within the bound.
No kernel may reach another device: no remote copies, remote signals or barrier semaphores. Data moves between devices by JAX's collectives and lax.ppermute only.
A program may use at most 256 MiB of HBM per device.

```python
import jax
import jax.numpy as jnp
from jax import lax

D = 2048
HEADS = 16
HEAD = 128
FF = 6144
WINDOW = 1024
BLOCK = 256
MIN_SEQ = 4
BLK_DEV = 2
NBLK = 16
TOKENS = 4096
NSEQ = 2
MOST = 12
N_DP = 8


def draw_sequence_blocks(key, part):
    grow_key = jax.random.fold_in(key, 11)
    order_key = jax.random.fold_in(key, 23)
    others = jnp.full((NSEQ - 1,), MIN_SEQ, dtype=jnp.int32)
    spare = NBLK - MOST - MIN_SEQ * (NSEQ - 1)

    def grow(step, lengths):
        scores = jax.random.randint(jax.random.fold_in(grow_key, step), (NSEQ - 1,), 0, 1 << 20) * NSEQ
        scores = scores + jnp.arange(NSEQ - 1, dtype=jnp.int32)
        scores = jnp.where(lengths < MOST, scores, -1)
        chosen = jnp.argmax(scores)
        return lengths.at[chosen].add(1)
    others = lax.fori_loop(0, spare, grow, others)
    lengths = jnp.concatenate([jnp.full((1,), MOST, dtype=jnp.int32), others])
    order = jax.random.permutation(order_key, NSEQ)
    return lengths[order].astype(jnp.int32)


def steps_of(key, dims, cuts, least, largest):
    loudness, own = 1.0, jax.random.fold_in(key, 6)
    for axis_at, shards_of in cuts:
        steps = jnp.exp(jax.random.uniform(jax.random.fold_in(own, axis_at), (shards_of,), jnp.float32, least / len(cuts), largest / len(cuts)))
        loudness = loudness * jnp.repeat(steps, dims[axis_at] // shards_of).reshape([-1 if axis == axis_at else 1 for axis in range(len(dims))])
    return loudness


def centred(stream_key, shape, deviation, most, split=(), kind=jnp.bfloat16):
    values = deviation * jax.random.normal(stream_key, shape, jnp.float32)
    if split:
        values = values * steps_of(stream_key, shape, split, -0.22, 0.18)
    return jnp.clip(values, -most, most).astype(kind)


def setup_inputs(seed: int = 0) -> dict:
    arg_keys = jax.random.split(jax.random.key(seed), 12)
    return {
        "block_input": centred(arg_keys[0], (TOKENS, D), 1.0, 6.0, ((0, 32),)),
        "cotangent": centred(arg_keys[1], (TOKENS, D), 1.0, 6.0, ((0, 32),)),
        "sequence_blocks": draw_sequence_blocks(jax.random.fold_in(arg_keys[11], 71), 0),
        "gain_attention": jnp.clip(1.0 + 0.1 * jax.random.normal(arg_keys[3], (D,), jnp.float32), 0.5, 1.5),
        "query_weight": centred(arg_keys[4], (D, HEADS * HEAD), D ** -0.5, 0.125, ((1, 4),)),
        "keyval_weight": centred(arg_keys[5], (D, 2 * HEAD), D ** -0.5, 0.125),
        "output_weight": centred(arg_keys[6], (D, HEADS * HEAD), (max(1, HEADS * HEAD // 256)) ** -0.5, 2.0, ((1, 4),)),
        "gain_feedforward": jnp.clip(1.0 + 0.1 * jax.random.normal(arg_keys[7], (D,), jnp.float32), 0.5, 1.5),
        "gate_weight": centred(arg_keys[8], (D, FF), D ** -0.5, 0.125, ((1, 4),)),
        "up_weight": centred(arg_keys[9], (D, FF), D ** -0.5, 0.125, ((1, 4),)),
        "down_weight": centred(arg_keys[10], (D, FF), FF ** -0.5, 0.078125, ((1, 4),)),
    }


@jax.custom_vjp
def low(v):
    return lax.optimization_barrier(v.astype(jnp.bfloat16)).astype(jnp.float32)

@jax.custom_vjp
def low_back(v):
    return v

def low_keep(v):
    return (low(v), None)

def low_pass(kept, grad):
    return (grad,)

def back_keep(v):
    return (v, None)

def back_low(kept, grad):
    return (low(grad),)
low.defvjp(low_keep, low_pass)
low_back.defvjp(back_keep, back_low)
epsilon = 1e-06
negative = -1e+30
highest = lax.Precision.HIGHEST

def multiply(left, right):
    return jnp.dot(left, right, precision=highest, preferred_element_type=jnp.float32)

def normalize(values, gain):
    return values * lax.rsqrt(lax.optimization_barrier(jnp.mean(values * values, axis=-1, keepdims=True)) + epsilon) * gain

def rotate(values, cosine, sine_table):
    half = values.shape[-1] // 2
    first = values[..., :half]
    second = values[..., half:]
    return jnp.concatenate([first * cosine - second * sine_table, second * cosine + first * sine_table], axis=-1)

def reference(block_input, cotangent, sequence_blocks, gain_attention, query_weight, keyval_weight, output_weight, gain_feedforward, gate_weight, up_weight, down_weight):
    blocks = N_DP * BLK_DEV
    spans = WINDOW // BLOCK + 1
    total_rows = blocks * BLOCK
    scale = HEAD ** (-0.5)
    numbers = jnp.arange(blocks, dtype=jnp.int32)
    dealt_of = (numbers % BLK_DEV * N_DP + numbers // BLK_DEV).astype(jnp.int32)
    place_of = (numbers % N_DP * BLK_DEV + numbers // N_DP).astype(jnp.int32)

    def to_initial(array):
        return array.reshape(blocks, BLOCK, -1)[place_of].reshape(total_rows, -1)

    def to_dealt(array):
        return array.reshape(blocks, BLOCK, -1)[dealt_of].reshape(total_rows, -1)
    ends = jnp.cumsum(sequence_blocks).astype(jnp.int32)
    starts = lax.optimization_barrier(jnp.sum(jnp.where(ends[None, :] <= numbers[:, None], sequence_blocks[None, :], 0), axis=1)).astype(jnp.int32)
    positions = ((numbers - starts)[:, None] * BLOCK + jnp.arange(BLOCK, dtype=jnp.int32)[None, :]).reshape(total_rows).astype(jnp.float32)
    frequency = 10000.0 ** (-jnp.arange(HEAD // 2, dtype=jnp.float32) * 2.0 / HEAD)
    angles = positions[:, None] * frequency[None, :]
    cosine = jnp.cos(angles)
    sine_table = jnp.sin(angles)
    row_index = jnp.arange(BLOCK, dtype=jnp.int32)[:, None]
    column_index = jnp.arange(spans * BLOCK, dtype=jnp.int32)[None, :]
    reach = column_index // BLOCK
    distance = reach * BLOCK + row_index - column_index % BLOCK
    inside = (distance >= 0) & (distance < WINDOW)

    def forward(inputs, gain_one, weight_query, weight_keyval, weight_output, gain_two, weight_gate, weight_up, weight_down):
        normed = low(normalize(inputs, gain_one))
        query_raw = low_back(multiply(normed, weight_query)).reshape(total_rows, HEADS, HEAD)
        queries = low(rotate(query_raw, cosine[:, None, :], sine_table[:, None, :]))
        keyval = multiply(normed, weight_keyval)
        keys = low(rotate(low_back(keyval[:, :HEAD]), cosine, sine_table))
        values = low(low_back(keyval[:, HEAD:]))
        padding = jnp.zeros(((spans - 1) * BLOCK, HEAD), jnp.float32)
        key_pad = jnp.concatenate([padding, keys], axis=0).reshape(blocks + spans - 1, BLOCK, HEAD)
        value_pad = jnp.concatenate([padding, values], axis=0).reshape(blocks + spans - 1, BLOCK, HEAD)
        query_blocks = queries.reshape(blocks, BLOCK, HEADS, HEAD)

        def attend(pack):
            number, start, query_block = pack
            picks = (number + spans - 1 - jnp.arange(spans, dtype=jnp.int32)).astype(jnp.int32)
            window_keys = jnp.take(key_pad, picks, axis=0).reshape(spans * BLOCK, HEAD)
            window_values = jnp.take(value_pad, picks, axis=0).reshape(spans * BLOCK, HEAD)
            scores = low_back(jnp.einsum('qhd,kd->hqk', query_block, window_keys, precision=highest) * scale)
            allowed = inside & (number - reach >= start)
            scores = jnp.where(allowed[None], scores, negative)
            peak = lax.optimization_barrier(jnp.max(scores, axis=-1, keepdims=True))
            exponent = jnp.exp(scores - peak)
            weights_soft = exponent / lax.optimization_barrier(jnp.sum(exponent, axis=-1, keepdims=True))
            return jnp.einsum('hqk,kd->qhd', low(weights_soft), window_values, precision=highest)
        attended = lax.map(jax.checkpoint(attend), (numbers, starts, query_blocks))
        attended = low(low_back(attended.reshape(total_rows, HEADS * HEAD)))
        hidden = inputs + low_back(multiply(attended, weight_output.T))
        normed_two = low(normalize(hidden, gain_two))
        gate = low_back(multiply(normed_two, weight_gate))
        upper = low_back(multiply(normed_two, weight_up))
        product = low(jax.nn.gelu(gate, approximate=True) * upper)
        return hidden + multiply(product, weight_down.T)
    arguments = (to_initial(block_input.astype(jnp.float32)), gain_attention.astype(jnp.float32), query_weight.astype(jnp.float32), keyval_weight.astype(jnp.float32), output_weight.astype(jnp.float32), gain_feedforward.astype(jnp.float32), gate_weight.astype(jnp.float32), up_weight.astype(jnp.float32), down_weight.astype(jnp.float32))
    result, backward = jax.vjp(forward, *arguments)
    grads = backward(to_initial(cotangent.astype(jnp.float32)))
    block_output = to_dealt(result).astype(jnp.bfloat16)
    grad_input = to_dealt(grads[0])
    return (block_output, grad_input, grads[1], grads[2], grads[3], grads[4], grads[5], grads[6], grads[7], grads[8])
```

```python
import jax
import jax.numpy as jnp
from jax import lax
from jax.sharding import PartitionSpec as P

HEAD = 128
WINDOW = 1024
BLOCK = 256
SPANS = WINDOW // BLOCK + 1

epsilon = 1e-06
negative = -1e30
low_type = jnp.bfloat16


def matmul(left, right):
    return jnp.dot(left, right, preferred_element_type=jnp.float32)


def times_transposed(left, right):
    return lax.dot_general(
        left, right, (((1,), (1,)), ((), ())), preferred_element_type=jnp.float32
    )


def outer_sum(left, right):
    return lax.dot_general(
        left, right, (((0,), (0,)), ((), ())), preferred_element_type=jnp.float32
    )


def flip(value, axis, bit):
    count = lax.axis_size(axis)
    return lax.ppermute(value, axis, [(i, i ^ bit) for i in range(count)])


def shift(value, step):
    count = lax.axis_size("dp")
    return lax.ppermute(value, "dp", [(i, (i + step) % count) for i in range(count)])


def gather_tensor(value):
    over = flip(value, "tensor", 2)
    return [value, flip(value, "tensor", 1), over, flip(over, "tensor", 1)]


def scatter_tensor(front, back):
    rows = front.shape[0] // 2
    far = back[:rows] + flip(back[rows:].astype(low_type), "tensor", 1)
    near = front[:rows] + flip(front[rows:].astype(low_type), "tensor", 1)
    return near + flip(far.astype(low_type), "tensor", 2)


def bit_of(index, bit):
    return (index >> bit) & 1


def pick(value, axis, index):
    return lax.dynamic_index_in_dim(value, index, axis, keepdims=False)


def reduce_weight(pairs, order, dp):
    count = lax.axis_size("dp")
    bits = sorted(order, reverse=True)
    lefts = []
    for left, _ in pairs:
        lefts.append(left.reshape(left.shape[0], *([2] * len(bits)), -1))
    rights = [right for _, right in pairs]
    size = lefts[0].shape[-1]
    width = rights[0].shape[1]
    pending = []

    def product(chosen, waiting):
        total = None
        for left, right in zip(chosen, rights):
            part = outer_sum(left.reshape(left.shape[0], -1), right)
            total = part if total is None else total + part
        for item in waiting:
            total = total + item.reshape(total.shape).astype(jnp.float32)
        return total

    for bit in order:
        place = bits.index(bit)
        mine = bit_of(dp, bit)
        away = product(
            [pick(left, place + 1, 1 - mine) for left in lefts],
            [pick(item, place, 1 - mine) for item in pending],
        ).astype(low_type)
        arrived = flip(away, "dp", 1 << bit)
        bits.remove(bit)
        lefts = [pick(left, place + 1, mine) for left in lefts]
        pending = [pick(item, place, mine) for item in pending]
        pending.append(arrived.reshape(*([2] * len(bits)), size, width))
    return product(lefts, pending)


def rotate(values, cosine, sine):
    half = values.shape[-1] // 2
    first = values[..., :half]
    second = values[..., half:]
    return jnp.concatenate(
        [first * cosine - second * sine, second * cosine + first * sine], axis=-1
    )


def gelu_parts(gate):
    root = 0.7978845608028654
    square = gate * gate
    curve = jnp.tanh(root * gate * (1.0 + 0.044715 * square))
    half = 0.5 * (1.0 + curve)
    slope = half + 0.5 * gate * (1.0 - curve * curve) * root * (1.0 + 3 * 0.044715 * square)
    return gate * half, slope


def per_device(
    block_input,
    cotangent,
    sequence_blocks,
    gain_attention,
    query_weight,
    keyval_weight,
    output_weight,
    gain_feedforward,
    gate_weight,
    up_weight,
    down_weight,
):
    count = lax.axis_size("dp")
    bits = count.bit_length() - 1
    dp = lax.axis_index("dp")
    rank = lax.axis_index("tensor")
    slot = rank >> 1
    side = rank & 1
    rows = block_input.shape[0]
    width = block_input.shape[1]
    heads = query_weight.shape[1] // HEAD
    scale = HEAD ** (-0.5)
    top = bits - 1
    half_width = width // 2
    half_start = bit_of(dp, top) * half_width

    def positions_of(number, offsets):
        ends = jnp.sum(
            jnp.where(
                jnp.arange(sequence_blocks.shape[0])[:, None]
                >= jnp.arange(sequence_blocks.shape[0])[None, :],
                sequence_blocks[None, :],
                0,
            ),
            axis=1,
        )
        start = jnp.sum(jnp.where(ends <= number, sequence_blocks, 0))
        return start, ((number - start) * BLOCK + offsets).astype(jnp.float32)

    def tables(position):
        frequency = 10000.0 ** (-jnp.arange(HEAD // 2, dtype=jnp.float32) * 2.0 / HEAD)
        angles = position[:, None] * frequency[None, :]
        return jnp.cos(angles), jnp.sin(angles)

    place = jnp.arange(rows, dtype=jnp.int32)
    both_sides = jnp.concatenate([side * rows + place, (1 - side) * rows + place])
    numbers = [dp + slot * count, dp + (1 - slot) * count]
    starts, cosines, sines = [], [], []
    for number in numbers:
        start, position = positions_of(number, both_sides)
        cosine, sine = tables(position)
        starts.append(start)
        cosines.append(cosine)
        sines.append(sine)
    own_cosine, own_sine = cosines[0][:rows], sines[0][:rows]
    cosine_all = jnp.concatenate(cosines)
    sine_all = jnp.concatenate(sines)

    own_input = block_input.astype(jnp.float32)
    factor_one = lax.rsqrt(jnp.mean(own_input * own_input, axis=-1, keepdims=True) + epsilon)
    scaled_one = own_input * factor_one
    own_normed = (scaled_one * gain_attention).astype(low_type)

    keyval = matmul(own_normed, keyval_weight)
    own_keyval = jnp.concatenate(
        [rotate(keyval[:, :HEAD], own_cosine, own_sine), keyval[:, HEAD:]], axis=1
    ).astype(low_type)
    near = [own_keyval] + [shift(own_keyval, k) for k in range(1, SPANS)]
    keyvals = gather_tensor(jnp.stack(near))
    keyvals = jnp.stack(
        [jnp.stack(keyvals[:2], axis=1), jnp.stack(keyvals[2:], axis=1)]
    )

    normed = jnp.concatenate(gather_tensor(own_normed))
    query_raw = matmul(normed, query_weight).reshape(4 * rows, heads, HEAD)
    queries = rotate(query_raw, cosine_all[:, None, :], sine_all[:, None, :]).astype(low_type)

    cotangent_far = flip(cotangent, "dp", 1 << top)
    cotangents = [
        jnp.concatenate(gather_tensor(cotangent)),
        jnp.concatenate(gather_tensor(cotangent_far)),
    ]

    sources = []
    windows = []
    allowed = []
    logs = []
    attended = []
    query_blocks = [
        queries[: 2 * rows].transpose(1, 0, 2),
        queries[2 * rows :].transpose(1, 0, 2),
    ]
    for u in range(2):
        is_late = (slot ^ u) == 1
        from_late = [is_late & (dp >= k) for k in range(SPANS)]
        from_other = [(late != (slot == 1)) for late in from_late]
        sources.append(from_other)
        window = jnp.concatenate(
            [
                jnp.where(from_other[k], keyvals[1, k], keyvals[0, k]).reshape(BLOCK, 2 * HEAD)
                for k in range(SPANS)
            ]
        )
        windows.append((window[:, :HEAD], window[:, HEAD:]))
        reach = jnp.repeat(jnp.arange(SPANS, dtype=jnp.int32), BLOCK)
        key_offset = reach * BLOCK - jnp.tile(both_sides, SPANS)
        distance = both_sides[:, None] + key_offset[None, :]
        mask = (distance >= 0) & (distance < WINDOW)
        mask = mask & ((numbers[u] - reach) >= starts[u])[None, :]
        allowed.append(mask)
        scores = (
            jnp.einsum(
                "hqd,kd->hqk",
                query_blocks[u],
                windows[u][0],
                preferred_element_type=jnp.float32,
            )
            * scale
        )
        scores = jnp.where(mask[None], scores, negative)
        peak = jnp.max(scores, axis=-1, keepdims=True)
        exponent = jnp.exp(scores - peak)
        total = jnp.sum(exponent, axis=-1, keepdims=True)
        soft = (exponent / total).astype(low_type)
        logs.append(peak + jnp.log(total))
        attended.append(
            jnp.einsum(
                "hqk,kd->hqd", soft, windows[u][1], preferred_element_type=jnp.float32
            )
            .transpose(1, 0, 2)
            .reshape(2 * rows, heads * HEAD)
            .astype(low_type)
        )
    own_hidden = own_input + scatter_tensor(
        *[times_transposed(item, output_weight) for item in attended]
    )
    factor_two = lax.rsqrt(jnp.mean(own_hidden * own_hidden, axis=-1, keepdims=True) + epsilon)
    scaled_two = own_hidden * factor_two
    own_normed_two = (scaled_two * gain_feedforward).astype(low_type)
    normed_two = [jnp.concatenate(gather_tensor(own_normed_two))]
    far_normed_two = flip(own_normed_two, "dp", 1 << top)

    def feed(rows_normed, rows_cotangent):
        gate = matmul(rows_normed, gate_weight)
        upper = matmul(rows_normed, up_weight)
        grad = matmul(rows_cotangent, down_weight)
        activated, slope = gelu_parts(gate)
        hidden = (activated * upper).astype(low_type)
        grad_gate = (grad * upper * slope).astype(low_type)
        grad_up = (grad * activated).astype(low_type)
        return hidden, grad_gate, grad_up

    fed = [feed(normed_two[0], cotangents[0])]
    hidden, grad_gate, grad_up = fed[0]
    grad_two = times_transposed(grad_gate, gate_weight) + times_transposed(grad_up, up_weight)
    own_grad_two = scatter_tensor(grad_two[: 2 * rows], grad_two[2 * rows :])
    grad_scaled = own_grad_two * gain_feedforward
    inner = jnp.mean(grad_scaled * scaled_two, axis=-1, keepdims=True)
    own_grad_hidden = cotangent.astype(jnp.float32) + factor_two * (
        grad_scaled - scaled_two * inner
    )
    grad_attention = jnp.concatenate(gather_tensor(own_grad_hidden.astype(low_type)))
    grad_attended = matmul(grad_attention, output_weight).astype(low_type)

    normed_two.append(jnp.concatenate(gather_tensor(far_normed_two)))
    fed.append(feed(normed_two[1], cotangents[1]))
    down_rows = times_transposed(hidden, down_weight)
    block_output = (own_hidden + scatter_tensor(down_rows[: 2 * rows], down_rows[2 * rows :])).astype(
        low_type
    )

    def half(value):
        return lax.dynamic_slice_in_dim(value, half_start, half_width, 1)

    half_normed_two = [half(item) for item in normed_two]
    half_cotangents = [half(item) for item in cotangents]
    low_order = list(range(top))
    grad_down = reduce_weight(
        [(half_cotangents[i], fed[i][0]) for i in range(2)], low_order, dp
    )
    grad_gate_weight = reduce_weight(
        [(half_normed_two[i], fed[i][1]) for i in range(2)], low_order[::-1], dp
    )
    grad_up_weight = reduce_weight(
        [(half_normed_two[i], fed[i][2]) for i in range(2)], low_order, dp
    )
    attended_all = jnp.concatenate(attended)
    grad_output_weight = reduce_weight(
        [(grad_attention, attended_all)], [*low_order[::-1], top], dp
    )

    grad_query_list = []
    returns = [[0.0] * SPANS, [0.0] * SPANS]
    for u in range(2):
        grad_block = (
            grad_attended[u * 2 * rows : (u + 1) * 2 * rows]
            .reshape(2 * rows, heads, HEAD)
            .transpose(1, 0, 2)
        )
        window_keys, window_values = windows[u]
        scores = (
            jnp.einsum(
                "hqd,kd->hqk", query_blocks[u], window_keys, preferred_element_type=jnp.float32
            )
            * scale
        )
        scores = jnp.where(allowed[u][None], scores, negative)
        soft = jnp.exp(scores - logs[u])
        grad_soft = jnp.einsum(
            "hqd,kd->hqk", grad_block, window_values, preferred_element_type=jnp.float32
        )
        grad_scores = (
            soft * (grad_soft - jnp.sum(grad_soft * soft, axis=-1, keepdims=True))
        ).astype(low_type)
        grad_query_list.append(
            (
                jnp.einsum(
                    "hqk,kd->hqd", grad_scores, window_keys, preferred_element_type=jnp.float32
                )
                * scale
            ).transpose(1, 0, 2)
        )
        grad_keys = (
            jnp.einsum(
                "hqk,hqd->kd", grad_scores, query_blocks[u], preferred_element_type=jnp.float32
            )
            * scale
        )
        grad_values = jnp.einsum(
            "hqk,hqd->kd", soft.astype(low_type), grad_block, preferred_element_type=jnp.float32
        )
        grad_window = jnp.concatenate([grad_keys, grad_values], axis=1).reshape(
            SPANS, BLOCK, 2 * HEAD
        )
        for k in range(SPANS):
            for v in range(2):
                returns[v][k] += jnp.where(sources[u][k] == (v == 1), grad_window[k], 0.0)
    grad_query_low = (
        rotate(jnp.concatenate(grad_query_list), cosine_all[:, None, :], -sine_all[:, None, :])
        .reshape(4 * rows, heads * HEAD)
        .astype(low_type)
    )
    grad_one_part = times_transposed(grad_query_low, query_weight)
    returned = [
        jnp.stack(item).reshape(SPANS, 2, rows, 2 * HEAD).transpose(1, 0, 2, 3) for item in returns
    ]
    own_returns = scatter_tensor(*returned)[0]
    own_grad_keyval = own_returns[0]
    for k in range(1, SPANS):
        own_grad_keyval = own_grad_keyval + shift(own_returns[k].astype(low_type), -k)
    own_grad_keyval = jnp.concatenate(
        [rotate(own_grad_keyval[:, :HEAD], own_cosine, -own_sine), own_grad_keyval[:, HEAD:]],
        axis=1,
    ).astype(low_type)

    grad_query_weight = reduce_weight(
        [(normed, grad_query_low)], [*low_order, top], dp
    )
    own_grad_one = scatter_tensor(
        grad_one_part[: 2 * rows], grad_one_part[2 * rows :]
    ) + times_transposed(own_grad_keyval, keyval_weight)
    grad_scaled = own_grad_one * gain_attention
    inner = jnp.mean(grad_scaled * scaled_one, axis=-1, keepdims=True)
    grad_rows = own_grad_hidden + factor_one * (grad_scaled - scaled_one * inner)

    quarter = 2 * HEAD // 4
    grad_keyval = jnp.concatenate(gather_tensor(own_grad_keyval))
    part = lax.dynamic_slice_in_dim(grad_keyval, rank * quarter, quarter, 1)
    part = reduce_weight([(normed, part)], [*low_order, top], dp)
    pieces = jnp.stack(gather_tensor(part.T))
    order = [
        pick(pieces, 0, rank ^ g).reshape(quarter, -1) for g in range(4)
    ]
    grad_keyval_weight = jnp.concatenate(order).T

    size = width // count

    def own_block(value):
        return lax.dynamic_slice_in_dim(value, dp * size, size, 0)

    def sum_tensor(value):
        value = value + flip(value, "tensor", 1)
        return value + flip(value, "tensor", 2)

    gain_two = (
        sum_tensor(
            jnp.sum(own_block(gate_weight).astype(jnp.float32) * grad_gate_weight, axis=1)
            + jnp.sum(own_block(up_weight).astype(jnp.float32) * grad_up_weight, axis=1)
        )
        / own_block(gain_feedforward)
    )
    gain_one = (
        sum_tensor(jnp.sum(own_block(query_weight).astype(jnp.float32) * grad_query_weight, axis=1))
        + jnp.sum(own_block(keyval_weight).astype(jnp.float32) * grad_keyval_weight, axis=1)
    ) / own_block(gain_attention)
    return (
        block_output,
        grad_rows,
        gain_one,
        grad_query_weight,
        grad_keyval_weight,
        grad_output_weight,
        gain_two,
        grad_gate_weight,
        grad_up_weight,
        grad_down,
    )


def solution(mesh):
    placed = (
        P(("dp", "tensor"), None),
        P(("dp", "tensor"), None),
        P(),
        P(),
        P(None, "tensor"),
        P(),
        P(None, "tensor"),
        P(),
        P(None, "tensor"),
        P(None, "tensor"),
        P(None, "tensor"),
    )
    return jax.shard_map(
        per_device,
        mesh=mesh,
        in_specs=placed,
        out_specs=(
            P(("dp", "tensor"), None),
            P(("dp", "tensor"), None),
            P("dp"),
            P("dp", "tensor"),
            P("dp", None),
            P("dp", "tensor"),
            P("dp"),
            P("dp", "tensor"),
            P("dp", "tensor"),
            P("dp", "tensor"),
        ),
        check_vma=False,
    )
```

```python
import functools

import jax
import jax.numpy as jnp
from jax import lax
from jax.experimental import pallas as pl
from jax.experimental.pallas import tpu as pltpu
from jax.sharding import PartitionSpec as P

HEAD = 128
WINDOW = 1024
BLOCK = 256
SPANS = WINDOW // BLOCK + 1

epsilon = 1e-06
negative = -1e30
low_type = jnp.bfloat16


def matmul(left, right):
    return jnp.dot(left, right, preferred_element_type=jnp.float32)


def times_transposed(left, right):
    return lax.dot_general(
        left, right, (((1,), (1,)), ((), ())), preferred_element_type=jnp.float32
    )


def outer_sum(left, right):
    return lax.dot_general(
        left, right, (((0,), (0,)), ((), ())), preferred_element_type=jnp.float32
    )


def flip(value, axis, bit):
    count = lax.axis_size(axis)
    return lax.ppermute(value, axis, [(i, i ^ bit) for i in range(count)])


def shift(value, step):
    count = lax.axis_size("dp")
    return lax.ppermute(value, "dp", [(i, (i + step) % count) for i in range(count)])


def gather_tensor(value):
    over = flip(value, "tensor", 2)
    return [value, flip(value, "tensor", 1), over, flip(over, "tensor", 1)]


def bit_of(index, bit):
    return (index >> bit) & 1


def pick(value, axis, index):
    return lax.dynamic_index_in_dim(value, index, axis, keepdims=False)


def reduce_weight_plain(pairs, order, dp):
    count = lax.axis_size("dp")
    bits = sorted(order, reverse=True)
    lefts = []
    for left, _ in pairs:
        lefts.append(left.reshape(left.shape[0], *([2] * len(bits)), -1))
    rights = [right for _, right in pairs]
    size = lefts[0].shape[-1]
    width = rights[0].shape[1]
    pending = []

    def product(chosen, waiting):
        total = None
        for left, right in zip(chosen, rights):
            part = outer_sum(left.reshape(left.shape[0], -1), right)
            total = part if total is None else total + part
        for item in waiting:
            total = total + item.reshape(total.shape).astype(jnp.float32)
        return total

    for bit in order:
        place = bits.index(bit)
        mine = bit_of(dp, bit)
        away = product(
            [pick(left, place + 1, 1 - mine) for left in lefts],
            [pick(item, place, 1 - mine) for item in pending],
        ).astype(low_type)
        arrived = flip(away, "dp", 1 << bit)
        bits.remove(bit)
        lefts = [pick(left, place + 1, mine) for left in lefts]
        pending = [pick(item, place, mine) for item in pending]
        pending.append(arrived.reshape(*([2] * len(bits)), size, width))
    return product(lefts, pending)


vmem_limit = 16 * 2**20
log2e = 1.4426950408889634
whole_vmem = pl.BlockSpec(memory_space=pltpu.VMEM)
whole_smem = pl.BlockSpec(memory_space=pltpu.SMEM)


def after(value, *others):
    return lax.optimization_barrier((value, *others))[0]


def cost(flops, transcendentals, *arrays):
    total = 0
    for item in arrays:
        total += item.size * item.dtype.itemsize
    return pl.CostEstimate(
        flops=int(flops), transcendentals=int(transcendentals), bytes_accessed=int(total)
    )


def parameters(limit=vmem_limit):
    return pltpu.CompilerParams(vmem_limit_bytes=limit)


def shape_of(shape, dtype):
    return jax.ShapeDtypeStruct(shape, dtype)


def turn(values, cosine, sine):
    return values * cosine + pltpu.roll(values, HEAD // 2, 1) * sine


def slot_facts(here, lengths, u, count):
    dp = here[0]
    slot = here[1] ^ u
    number = dp + slot * count
    start = jnp.int32(0)
    end = jnp.int32(0)
    for n in range(lengths.shape[0]):
        end = end + lengths[n]
        start = jnp.where(end <= number, end, start)
    pairs = [
        (slot if k == 0 else jnp.where(dp >= k, slot, 0)) ^ here[1] for k in range(SPANS)
    ]
    return number - start, pairs


def angle_tables(block, side, frequency, rows):
    place = lax.broadcasted_iota(jnp.int32, (rows, HEAD), 0) ^ (side * (BLOCK // 2))
    lane = lax.broadcasted_iota(jnp.int32, (rows, HEAD), 1)
    angle = (block * BLOCK + place).astype(jnp.float32) * frequency
    sine = jnp.sin(angle)
    return jnp.cos(angle), jnp.where(lane < HEAD // 2, -sine, sine)


def opening_kernel(
    here, lengths, x_ref, gain_ref, weight_ref, frequency_ref, normed_ref, keyval_ref, *, count
):
    x = x_ref[...].astype(jnp.float32)
    factor = lax.rsqrt(jnp.mean(x * x, axis=-1, keepdims=True) + epsilon)
    normed = (x * factor * gain_ref[...]).astype(low_type)
    normed_ref[...] = normed
    keyval = matmul(normed, weight_ref[...])
    block, _ = slot_facts(here, lengths, 0, count)
    cosine, sine = angle_tables(block, here[2], frequency_ref[...], x.shape[0])
    keyval_ref[:, :HEAD] = turn(keyval[:, :HEAD], cosine, sine).astype(low_type)
    keyval_ref[:, HEAD:] = keyval[:, HEAD:].astype(low_type)


def opening(here, lengths, x, gain, weight, frequency, count):
    outs = (
        shape_of(x.shape, low_type),
        shape_of((x.shape[0], weight.shape[1]), low_type),
    )
    return pl.pallas_call(
        functools.partial(opening_kernel, count=count),
        out_shape=outs,
        in_specs=[whole_smem] * 2 + [whole_vmem] * 4,
        out_specs=(whole_vmem, whole_vmem),
        compiler_params=parameters(),
        cost_estimate=cost(2 * x.size * weight.shape[1], x.shape[0], x, weight, *outs),
        name="opening",
    )(here, lengths, x, gain.reshape(1, -1), weight, frequency)


def tables_kernel(here, lengths, frequency_ref, normed_ref, cosine_ref, sine_ref, *, count):
    del normed_ref
    for u in range(2):
        block, _ = slot_facts(here, lengths, u, count)
        cosine, sine = angle_tables(block, here[2], frequency_ref[...], BLOCK)
        cosine_ref[u] = cosine
        sine_ref[u] = sine


def tables(here, lengths, frequency, earlier, count):
    out = shape_of((2, BLOCK, HEAD), jnp.float32)
    return pl.pallas_call(
        functools.partial(tables_kernel, count=count),
        out_shape=(out, out),
        in_specs=[whole_smem] * 2 + [whole_vmem, pl.BlockSpec(memory_space=pl.ANY)],
        out_specs=(whole_vmem, whole_vmem),
        compiler_params=parameters(),
        cost_estimate=cost(100 * out.size, 0, out, out),
        name="tables",
    )(here, lengths, frequency, earlier)


def project_kernel(normed_a, normed_b, weight_ref, cosine_ref, sine_ref, query_ref, *, u):
    normed = jnp.concatenate([normed_a[...], normed_b[...]], axis=0)
    raw = matmul(normed, weight_ref[...])
    for head in range(raw.shape[1] // HEAD):
        at = slice(head * HEAD, (head + 1) * HEAD)
        query_ref[:, at] = turn(raw[:, at], cosine_ref[u], sine_ref[u]).astype(low_type)


def project(normed, weight, cosine, sine, u):
    rows, width = normed[0].shape
    columns = weight.shape[1]
    out = shape_of((2 * rows, columns), low_type)
    return pl.pallas_call(
        functools.partial(project_kernel, u=u),
        out_shape=out,
        in_specs=[whole_vmem] * 5,
        out_specs=whole_vmem,
        compiler_params=parameters(),
        cost_estimate=cost(4 * rows * width * columns, 0, *normed, weight, out),
        name="project",
    )(*normed, weight, cosine, sine)


def stack_kernel(*refs):
    *parts, out_ref = refs
    for k, part in enumerate(parts):
        out_ref[k] = part[...]


def stack(parts):
    out = shape_of((len(parts), *parts[0].shape), parts[0].dtype)
    return pl.pallas_call(
        stack_kernel,
        out_shape=out,
        in_specs=[whole_vmem] * len(parts),
        out_specs=whole_vmem,
        compiler_params=parameters(),
        cost_estimate=cost(0, 0, out, out),
        name="stack",
    )(*parts)


def fill_window(pairs, keyvals, keys, values):
    half = BLOCK // 2
    for k in range(SPANS):
        for side in range(2):
            block = keyvals[side][k, pairs[k]]
            at = k * BLOCK + side * half
            keys[at : at + half, :] = block[:, :HEAD]
            values[at : at + half, :] = block[:, HEAD:]


def window_masks(block, side):
    swap = side * (BLOCK // 2)
    keys = lax.broadcasted_iota(jnp.int32, (BLOCK, BLOCK), 0) ^ swap
    rows = lax.broadcasted_iota(jnp.int32, (BLOCK, BLOCK), 1) ^ swap
    beyond = jnp.where(block >= SPANS - 1, 0, BLOCK)
    return keys <= rows, keys > rows + beyond


def masked(scores, k, masks, block):
    if k == 0:
        return jnp.where(masks[0], scores, negative)
    if k == SPANS - 1:
        return jnp.where(masks[1], scores, negative)
    return scores + jnp.where(block >= k, 0.0, negative)


def attend_kernel(
    here,
    lengths,
    query_ref,
    output_weight,
    keyval_0,
    keyval_1,
    even_ref,
    odd_ref,
    attended_ref,
    log_ref,
    keys,
    values,
    *,
    heads,
    u,
    count,
):
    block, pairs = slot_facts(here, lengths, u, count)
    fill_window(pairs, (keyval_0, keyval_1), keys, values)
    masks = window_masks(block, here[2])
    values_turned = values[...].T
    factor = HEAD ** (-0.5) * log2e
    for head in range(heads):
        at = slice(head * HEAD, (head + 1) * HEAD)
        query = query_ref[:, at]
        scores = []
        for k in range(SPANS):
            part = times_transposed(keys[k * BLOCK : (k + 1) * BLOCK, :], query) * factor
            scores.append(masked(part, k, masks, block))
        peak = jnp.max(scores[0], axis=0, keepdims=True)
        for part in scores[1:]:
            peak = jnp.maximum(peak, jnp.max(part, axis=0, keepdims=True))
        exponents = [jnp.exp2(part - peak) for part in scores]
        total = jnp.sum(exponents[0], axis=0, keepdims=True)
        for part in exponents[1:]:
            total = total + jnp.sum(part, axis=0, keepdims=True)
        inverse = 1.0 / total
        log_ref[head : head + 1, :] = peak + jnp.log(total) * log2e
        soft = jnp.concatenate([(part * inverse).astype(low_type) for part in exponents], axis=0)
        attended_ref[:, at] = matmul(values_turned, soft).T.astype(low_type)
    part = times_transposed(attended_ref[...], output_weight[...]).astype(low_type)
    even_ref[...] = part[: BLOCK // 2]
    odd_ref[...] = part[BLOCK // 2 :]


def attend(here, lengths, query, output_weight, keyvals, u, count):
    width, columns = output_weight.shape
    heads = columns // HEAD
    outs = (
        shape_of((BLOCK // 2, width), low_type),
        shape_of((BLOCK // 2, width), low_type),
        shape_of((BLOCK, columns), low_type),
        shape_of((8, BLOCK), jnp.float32),
    )
    flops = 2 * BLOCK * width * columns + 4 * BLOCK * SPANS * BLOCK * columns
    return pl.pallas_call(
        functools.partial(attend_kernel, heads=heads, u=u, count=count),
        out_shape=outs,
        in_specs=[whole_smem] * 2 + [whole_vmem] * 4,
        out_specs=(whole_vmem,) * 4,
        scratch_shapes=[pltpu.VMEM((SPANS * BLOCK, HEAD), low_type)] * 2,
        compiler_params=parameters(),
        cost_estimate=cost(
            flops, heads * SPANS * BLOCK * BLOCK, output_weight, *keyvals, *outs
        ),
        name="attend",
    )(here, lengths, query, output_weight, *keyvals)


def retreat_kernel(
    here,
    lengths,
    grad_a,
    grad_b,
    query_weight,
    output_weight,
    keyval_0,
    keyval_1,
    cosine_ref,
    sine_ref,
    query_ref,
    attended_ref,
    log_ref,
    *rest,
    heads,
    closing,
    u,
    count,
):
    block, pairs = slot_facts(here, lengths, u, count)
    if closing:
        other_keys, other_values = rest[:2]
        rest = rest[2:]
        even_ref, odd_ref, grad_query_ref, keep_0, keep_2, away = rest[:6]
        rest = rest[6:]
    else:
        even_ref, odd_ref, grad_query_ref, grad_keys, grad_values = rest[:5]
        rest = rest[5:]
    keys, values = rest[:2]
    if closing:
        grad_keys, grad_values = rest[2:4]
    fill_window(pairs, (keyval_0, keyval_1), keys, values)
    masks = window_masks(block, here[2])
    grad = jnp.concatenate([grad_a[...], grad_b[...]], axis=0)
    grad_attended = matmul(grad, output_weight[...]).astype(low_type)
    keys_turned = keys[...].T
    scale = HEAD ** (-0.5)
    factor = scale * log2e
    for head in range(heads):
        at = slice(head * HEAD, (head + 1) * HEAD)
        query = query_ref[:, at]
        grad_head = grad_attended[:, at]
        inner = jnp.sum(
            (grad_head.astype(jnp.float32) * attended_ref[:, at].astype(jnp.float32)).T,
            axis=0,
            keepdims=True,
        )
        log_row = log_ref[head : head + 1, :]
        grad_query = None
        for k in range(SPANS):
            span = slice(k * BLOCK, (k + 1) * BLOCK)
            part = times_transposed(keys[span, :], query) * factor
            soft = jnp.exp2(masked(part, k, masks, block) - log_row)
            grad_soft = times_transposed(values[span, :], grad_head)
            grad_scores = (soft * (grad_soft - inner)).astype(low_type)
            grad_key = matmul(grad_scores, query)
            grad_value = matmul(soft.astype(low_type), grad_head)
            if head == 0:
                grad_keys[span, :] = grad_key
                grad_values[span, :] = grad_value
            else:
                grad_keys[span, :] += grad_key
                grad_values[span, :] += grad_value
            step = matmul(keys_turned[:, span], grad_scores)
            grad_query = step if grad_query is None else grad_query + step
        grad_query_ref[:, at] = turn(
            grad_query.T * scale, cosine_ref[u], -sine_ref[u]
        ).astype(low_type)
    part = times_transposed(grad_query_ref[...], query_weight[...]).astype(low_type)
    even_ref[...] = part[: BLOCK // 2]
    odd_ref[...] = part[BLOCK // 2 :]
    if closing:
        _, other_pairs = slot_facts(here, lengths, 1 - u, count)
        half = BLOCK // 2
        for k in range(SPANS):
            for pair in range(2):
                mine = jnp.where(pairs[k] == pair, 1.0, 0.0)
                other = jnp.where(other_pairs[k] == pair, 1.0, 0.0)
                for side in range(2):
                    span = slice(k * BLOCK + side * half, k * BLOCK + (side + 1) * half)
                    key = (grad_keys[span, :] * mine + other_keys[span, :] * other) * scale
                    value = grad_values[span, :] * mine + other_values[span, :] * other
                    if side == 1:
                        away[pair, k, :, :HEAD] = key.astype(low_type)
                        away[pair, k, :, HEAD:] = value.astype(low_type)
                    else:
                        keep = keep_2 if pair else keep_0
                        keep[k, :, :HEAD] = key
                        keep[k, :, HEAD:] = value


def retreat(
    here,
    lengths,
    grads,
    query_weight,
    output_weight,
    keyvals,
    cosine,
    sine,
    query,
    attended,
    logs,
    other,
    u,
    count,
):
    rows, width = grads[0].shape
    columns = query_weight.shape[1]
    heads = columns // HEAD
    closing = other is not None
    outs = [
        shape_of((rows, width), low_type),
        shape_of((rows, width), low_type),
        shape_of((BLOCK, columns), low_type),
    ]
    window = (SPANS * BLOCK, HEAD)
    scratch = [pltpu.VMEM(window, low_type)] * 2
    operands = [
        here, lengths, *grads, query_weight, output_weight, *keyvals, cosine, sine, query,
        attended, logs,
    ]
    in_specs = [whole_smem] * 2 + [whole_vmem] * 11
    if closing:
        outs += [
            shape_of((SPANS, rows, 2 * HEAD), jnp.float32),
            shape_of((SPANS, rows, 2 * HEAD), jnp.float32),
            shape_of((2, SPANS, rows, 2 * HEAD), low_type),
        ]
        scratch += [pltpu.VMEM(window, jnp.float32)] * 2
        operands += other
        in_specs += [whole_vmem] * 2
    else:
        outs += [shape_of(window, jnp.float32)] * 2
    flops = 4 * BLOCK * width * columns + 10 * BLOCK * SPANS * BLOCK * columns
    return pl.pallas_call(
        functools.partial(retreat_kernel, heads=heads, closing=closing, u=u, count=count),
        out_shape=tuple(outs),
        in_specs=in_specs,
        out_specs=(whole_vmem,) * len(outs),
        scratch_shapes=scratch,
        compiler_params=parameters(20 * 2**20),
        cost_estimate=cost(
            flops, heads * SPANS * BLOCK * BLOCK, query_weight, output_weight, *keyvals, *outs
        ),
        name="retreat",
    )(*operands)


def return_kernel(here, lengths, *refs, count):
    *parts, frequency_ref, own_ref, out_ref = refs
    total = own_ref[0]
    for part in parts:
        total = total + part[...].astype(jnp.float32)
    block, _ = slot_facts(here, lengths, 0, count)
    cosine, sine = angle_tables(block, here[2], frequency_ref[...], total.shape[0])
    out_ref[:, :HEAD] = turn(total[:, :HEAD], cosine, -sine).astype(low_type)
    out_ref[:, HEAD:] = total[:, HEAD:].astype(low_type)


def return_keyval(here, lengths, parts, frequency, own, count):
    out = shape_of(parts[0].shape, low_type)
    return pl.pallas_call(
        functools.partial(return_kernel, count=count),
        out_shape=out,
        in_specs=[whole_smem] * 2 + [whole_vmem] * (len(parts) + 2),
        out_specs=whole_vmem,
        compiler_params=parameters(),
        cost_estimate=cost(0, out.size, out, *parts, own),
        name="return_keyval",
    )(here, lengths, *parts, frequency, own)


def split_columns(columns):
    for size in (256, 128):
        if columns % size == 0:
            return size
    return columns


def grad_product_kernel(*refs):
    *parts, weight_ref, out_ref = refs
    rows = jnp.concatenate([part[...] for part in parts], axis=0)
    out_ref[...] = matmul(rows, weight_ref[...])


def grad_product(parts, weight):
    rows, width = parts[0].shape
    columns = weight.shape[1]
    tile = split_columns(columns)
    out = shape_of((rows * len(parts), columns), jnp.float32)
    return pl.pallas_call(
        grad_product_kernel,
        out_shape=out,
        grid=(columns // tile,),
        in_specs=[pl.BlockSpec((rows, width), lambda i: (0, 0))] * len(parts)
        + [pl.BlockSpec((width, tile), lambda i: (0, i))],
        out_specs=pl.BlockSpec((rows * len(parts), tile), lambda i: (0, i)),
        compiler_params=parameters(),
        cost_estimate=cost(2 * rows * len(parts) * width * columns, 0, *parts, weight, out),
        name="grad_product",
    )(*parts, weight)


def feed_kernel(*refs, count, closing):
    parts = refs[:count]
    grad_ref, gate_ref, up_ref = refs[count : count + 3]
    outs = refs[count + 3 :]
    hidden_ref, grad_gate_ref, grad_up_ref = outs[:3]
    rows = jnp.concatenate([part[...] for part in parts], axis=0)
    gate = matmul(rows, gate_ref[...])
    upper = matmul(rows, up_ref[...])
    grad = grad_ref[...]
    activated, slope = gelu_parts(gate)
    hidden_ref[...] = (activated * upper).astype(low_type)
    grad_gate = (grad * upper * slope).astype(low_type)
    grad_up = (grad * activated).astype(low_type)
    grad_gate_ref[...] = grad_gate
    grad_up_ref[...] = grad_up
    if closing:
        even_ref, odd_ref, total = outs[3:]
        step = times_transposed(grad_gate, gate_ref[...]) + times_transposed(
            grad_up, up_ref[...]
        )

        @pl.when(pl.program_id(0) == 0)
        def _():
            total[...] = step

        @pl.when(pl.program_id(0) > 0)
        def _():
            total[...] += step

        @pl.when(pl.program_id(0) == pl.num_programs(0) - 1)
        def _():
            size = even_ref.shape[0]
            even_ref[...] = total[:size].astype(low_type)
            odd_ref[...] = total[size:].astype(low_type)


def feed(parts, grad, grad_at, gate_weight, up_weight, closing):
    rows, width = parts[0].shape
    columns = gate_weight.shape[1]
    tile = split_columns(columns)
    total_rows = rows * len(parts)
    outs = [shape_of((total_rows, columns), low_type)] * 3
    tile_spec = pl.BlockSpec((total_rows, tile), lambda i: (0, i))
    out_specs = [tile_spec] * 3
    scratch = []
    whole = pl.BlockSpec((rows, width), lambda i: (0, 0))
    if closing:
        outs += [shape_of((rows, width), low_type)] * 2
        out_specs += [whole] * 2
        scratch = [pltpu.VMEM((total_rows, width), jnp.float32)]
    flops = (8 if closing else 4) * total_rows * width * columns
    return pl.pallas_call(
        functools.partial(feed_kernel, count=len(parts), closing=closing),
        out_shape=tuple(outs),
        grid=(columns // tile,),
        in_specs=[whole] * len(parts)
        + [pl.BlockSpec((total_rows, tile), lambda i: (grad_at, i))]
        + [pl.BlockSpec((width, tile), lambda i: (0, i))] * 2,
        out_specs=tuple(out_specs),
        scratch_shapes=scratch,
        compiler_params=parameters(),
        cost_estimate=cost(flops, total_rows * columns, gate_weight, up_weight, *outs, *outs[:1]),
        name="feed_back" if closing else "feed",
    )(*parts, grad, gate_weight, up_weight)


def weight_kernel(here, *refs, lefts, rights, waits):
    del here
    left = jnp.concatenate([ref[...] for ref in refs[:lefts]], axis=0)
    right = jnp.concatenate([ref[...] for ref in refs[lefts : lefts + rights]], axis=0)
    total = matmul(left.T, right)
    for ref in refs[lefts + rights : lefts + rights + waits]:
        total = total + ref[...].astype(jnp.float32)
    out_ref = refs[-1]
    out_ref[...] = total.astype(out_ref.dtype)


def weight_blocks(here, lefts, rights, fixed, free, waiting, size, dtype):
    blocks = 1 << len(free)
    columns = rights[0].shape[1]
    tokens = sum(item.shape[0] for item in rights)
    out = shape_of((blocks * size, columns), dtype)
    known = dict(fixed)

    def block_at(i, here, kept):
        total = 0
        for place, bit in enumerate(kept):
            if bit in known:
                value = ((here[0] >> bit) & 1) ^ known[bit]
            else:
                value = (i >> free.index(bit)) & 1
            total = total + (value << place)
        return total

    every = sorted([*known, *free])
    in_specs = [
        pl.BlockSpec((item.shape[0], size), lambda i, here: (0, block_at(i, here, every)))
        for item in lefts
    ]
    in_specs += [pl.BlockSpec(item.shape, lambda i, here: (0, 0)) for item in rights]
    for _, kept in waiting:
        in_specs.append(
            pl.BlockSpec(
                (size, columns),
                functools.partial(lambda i, here, kept: (block_at(i, here, kept), 0), kept=kept),
            )
        )
    arrays = [item for item, _ in waiting]
    return pl.pallas_call(
        functools.partial(
            weight_kernel, lefts=len(lefts), rights=len(rights), waits=len(waiting)
        ),
        out_shape=out,
        grid_spec=pltpu.PrefetchScalarGridSpec(
            num_scalar_prefetch=1,
            grid=(blocks,),
            in_specs=in_specs,
            out_specs=pl.BlockSpec((size, columns), lambda i, here: (i, 0)),
        ),
        compiler_params=parameters(),
        cost_estimate=cost(2 * tokens * blocks * size * columns, 0, out, *rights, *arrays),
        name="weight_blocks",
    )(here, *lefts, *rights, *arrays)


class WeightSum:
    def __init__(self, here, lefts, rights, order, fixed=()):
        self.here = here
        self.lefts = lefts
        self.rights = rights
        self.bits = list(order)
        self.known = [(bit, 0) for bit in fixed]
        self.waiting = []
        self.size = lefts[0].shape[1] // lax.axis_size("dp")
        self.plain = self.size % HEAD != 0
        self.fixed = fixed

    def send(self):
        bit = self.bits.pop(0)
        away = weight_blocks(
            self.here,
            self.lefts,
            self.rights,
            [*self.known, (bit, 1)],
            self.bits,
            self.waiting,
            self.size,
            low_type,
        )
        self.known.append((bit, 0))
        return away, bit

    def receive(self, away, bit):
        self.waiting.append((flip(away, "dp", 1 << bit), list(self.bits)))

    def step(self):
        if not self.plain:
            self.receive(*self.send())

    def finish(self):
        if not self.plain:
            return weight_blocks(
                self.here,
                self.lefts,
                self.rights,
                self.known,
                [],
                self.waiting,
                self.size,
                jnp.float32,
            )
        dp = lax.axis_index("dp")
        left = jnp.concatenate(self.lefts)
        for bit in self.fixed:
            left = left.reshape(left.shape[0], -1, 2, self.size << bit)
            left = pick(left, 2, bit_of(dp, bit)).reshape(left.shape[0], -1)
        return reduce_weight_plain(
            [(left, jnp.concatenate(self.rights))], self.bits, dp
        )


def gelu_parts(gate):
    root = 0.7978845608028654
    square = gate * gate
    curve = jnp.tanh(root * gate * (1.0 + 0.044715 * square))
    half = 0.5 * (1.0 + curve)
    slope = half + 0.5 * gate * (1.0 - curve * curve) * root * (1.0 + 3 * 0.044715 * square)
    return gate * half, slope


def norm_back(grad, scaled, factor, gain):
    grad_scaled = grad * gain
    inner = jnp.mean(grad_scaled * scaled, axis=-1, keepdims=True)
    return factor * (grad_scaled - scaled * inner)


def to_float(value):
    return value.astype(jnp.float32)


def per_device(
    block_input,
    cotangent,
    sequence_blocks,
    gain_attention,
    query_weight,
    keyval_weight,
    output_weight,
    gain_feedforward,
    gate_weight,
    up_weight,
    down_weight,
):
    count = lax.axis_size("dp")
    bits = count.bit_length() - 1
    dp = lax.axis_index("dp")
    rank = lax.axis_index("tensor")
    rows = block_input.shape[0]
    width = block_input.shape[1]
    top = bits - 1
    here = jnp.stack([dp, rank >> 1, rank & 1, rank]).astype(jnp.int32)
    lengths = sequence_blocks
    lane = jnp.arange(HEAD, dtype=jnp.float32) % (HEAD // 2)
    frequency = (10000.0 ** (-lane * 2.0 / HEAD))[None, :]

    own_normed, own_keyval = opening(
        here, lengths, block_input, gain_attention, keyval_weight, frequency, count
    )
    keyval_over = flip(own_keyval, "tensor", 2)
    cosine, sine = tables(here, lengths, frequency, own_keyval, count)
    own_normed = after(own_normed, cosine)
    normed = gather_tensor(own_normed)
    near = stack([own_keyval, keyval_over])
    spread = stack([near] + [shift(near, k) for k in range(1, SPANS)])
    across = flip(spread, "tensor", 1)
    keyvals = [spread, across]
    query_0 = project(normed[:2], query_weight, cosine, sine, 0)
    query_1 = project(normed[2:], query_weight, cosine, sine, 1)

    late_cotangent = after(cotangent, spread)
    cotangents = gather_tensor(late_cotangent)
    cotangent_far = flip(late_cotangent, "dp", 1 << top)

    even_1, odd_1, attended_1, logs_1 = attend(
        here, lengths, query_1, output_weight, keyvals, 1, count
    )
    even_0, odd_0, attended_0, logs_0 = attend(
        here, lengths, after(query_0, even_1), output_weight, keyvals, 0, count
    )

    def scatter(even_front, odd_front, even_back, odd_back):
        far = to_float(even_back) + to_float(flip(odd_back, "tensor", 1))
        near = to_float(even_front) + to_float(flip(odd_front, "tensor", 1))
        return near + to_float(flip(far.astype(low_type), "tensor", 2))

    own_input = to_float(block_input)
    own_hidden = own_input + scatter(even_0, odd_0, even_1, odd_1)
    factor_two = lax.rsqrt(jnp.mean(own_hidden * own_hidden, axis=-1, keepdims=True) + epsilon)
    scaled_two = own_hidden * factor_two
    own_normed_two = (scaled_two * gain_feedforward).astype(low_type)
    grad_hidden = grad_product(
        [after(cotangents[0], even_0), *cotangents[1:]], down_weight
    )
    normed_two = gather_tensor(own_normed_two)
    far_two = flip(own_normed_two, "dp", 1 << top)

    hidden_0, grad_gate_0, grad_up_0, back_even_0, back_odd_0 = feed(
        normed_two[:2], grad_hidden, 0, gate_weight, up_weight, True
    )
    hidden_1, grad_gate_1, grad_up_1, back_even_1, back_odd_1 = feed(
        [after(normed_two[2], back_even_0), normed_two[3]], grad_hidden, 1, gate_weight, up_weight, True
    )
    normed_two_far = gather_tensor(after(far_two, normed_two[2]))
    cotangents_far = gather_tensor(after(cotangent_far, own_normed_two))
    own_grad_two = scatter(back_even_0, back_odd_0, back_even_1, back_odd_1)
    own_grad_hidden = to_float(cotangent) + norm_back(
        own_grad_two, scaled_two, factor_two, gain_feedforward
    )
    own_grad_low = own_grad_hidden.astype(low_type)
    grad_attention = gather_tensor(own_grad_low)
    grad_hidden_far = grad_product(
        [after(cotangents_far[0], back_even_1), *cotangents_far[1:]], down_weight
    )
    hidden_far, grad_gate_far, grad_up_far = feed(
        normed_two_far, grad_hidden_far, 0, gate_weight, up_weight, False
    )

    both_normed_two = [*normed_two, *normed_two_far]
    low_order = list(range(top))
    down_sum = WeightSum(
        here,
        [*cotangents, *cotangents_far],
        [hidden_0, hidden_1, hidden_far],
        low_order[::-1],
        (top,),
    )
    gate_sum = WeightSum(
        here, both_normed_two, [grad_gate_0, grad_gate_1, grad_gate_far], low_order, (top,)
    )
    up_sum = WeightSum(
        here, both_normed_two, [grad_up_0, grad_up_1, grad_up_far], low_order, (top,)
    )
    sums = (gate_sum, down_sum, up_sum)
    for item in sums:
        item.step()

    back_even_0, back_odd_0, grad_query_0, window_keys, window_values = retreat(
        here,
        lengths,
        grad_attention[:2],
        query_weight,
        output_weight,
        keyvals,
        cosine,
        sine,
        query_0,
        attended_0,
        logs_0,
        None,
        0,
        count,
    )
    back_even_1, back_odd_1, grad_query_1, keep_0, keep_2, away = retreat(
        here,
        lengths,
        grad_attention[2:],
        query_weight,
        output_weight,
        keyvals,
        cosine,
        sine,
        query_1,
        attended_1,
        logs_1,
        [window_keys, window_values],
        1,
        count,
    )
    arrived = flip(away, "tensor", 1)
    far_returns = (keep_2 + to_float(arrived[1])).astype(low_type)
    own_returns = keep_0 + to_float(arrived[0]) + to_float(flip(far_returns, "tensor", 2))
    back = [shift(own_returns[k].astype(low_type), -k) for k in range(1, SPANS)]
    own_grad_keyval = return_keyval(here, lengths, back, frequency, own_returns[:1], count)

    for item in sums:
        for _ in range(len(item.bits)):
            item.step()
    grad_down = down_sum.finish()
    grad_gate_weight = gate_sum.finish()
    grad_up_weight = up_sum.finish()

    query_sum = WeightSum(here, normed, [grad_query_0, grad_query_1], [*low_order, top])
    output_sum = WeightSum(
        here, grad_attention, [attended_0, attended_1], [*low_order[::-1], top]
    )
    for _ in range(bits):
        query_sum.step()
    for _ in range(bits):
        output_sum.step()
    grad_query_weight = query_sum.finish()
    grad_output_weight = output_sum.finish()

    own_grad_one = scatter(back_even_0, back_odd_0, back_even_1, back_odd_1) + times_transposed(
        own_grad_keyval, keyval_weight
    )
    factor_one = lax.rsqrt(jnp.mean(own_input * own_input, axis=-1, keepdims=True) + epsilon)
    grad_rows = own_grad_hidden + norm_back(
        own_grad_one, own_input * factor_one, factor_one, gain_attention
    )

    quarter = 2 * HEAD // 4
    grad_keyval = jnp.concatenate(gather_tensor(own_grad_keyval))
    part = lax.dynamic_slice_in_dim(grad_keyval, rank * quarter, quarter, 1)
    keyval_sum = WeightSum(here, normed, [part], [*low_order, top])
    for _ in range(bits):
        keyval_sum.step()
    pieces = jnp.stack(gather_tensor(keyval_sum.finish().T))
    pieces = [pick(pieces, 0, rank ^ g).reshape(quarter, -1) for g in range(4)]
    grad_keyval_weight = jnp.concatenate(pieces).T

    down_front = times_transposed(hidden_0, down_weight).astype(low_type)
    down_back = times_transposed(hidden_1, down_weight).astype(low_type)
    block_output = (
        own_hidden
        + scatter(down_front[:rows], down_front[rows:], down_back[:rows], down_back[rows:])
    ).astype(low_type)

    size = width // count

    def own_block(value):
        return lax.dynamic_slice_in_dim(value, dp * size, size, 0)

    def sum_tensor(value):
        value = value + flip(value, "tensor", 1)
        return value + flip(value, "tensor", 2)

    gain_two = sum_tensor(
        jnp.sum(to_float(own_block(gate_weight)) * grad_gate_weight, axis=1)
        + jnp.sum(to_float(own_block(up_weight)) * grad_up_weight, axis=1)
    ) / own_block(gain_feedforward)
    gain_one = (
        sum_tensor(jnp.sum(to_float(own_block(query_weight)) * grad_query_weight, axis=1))
        + jnp.sum(to_float(own_block(keyval_weight)) * grad_keyval_weight, axis=1)
    ) / own_block(gain_attention)
    return (
        block_output,
        grad_rows,
        gain_one,
        grad_query_weight,
        grad_keyval_weight,
        grad_output_weight,
        gain_two,
        grad_gate_weight,
        grad_up_weight,
        grad_down,
    )


def solution(mesh):
    placed = (
        P(("dp", "tensor"), None),
        P(("dp", "tensor"), None),
        P(),
        P(),
        P(None, "tensor"),
        P(),
        P(None, "tensor"),
        P(),
        P(None, "tensor"),
        P(None, "tensor"),
        P(None, "tensor"),
    )
    return jax.shard_map(
        per_device,
        mesh=mesh,
        in_specs=placed,
        out_specs=(
            P(("dp", "tensor"), None),
            P(("dp", "tensor"), None),
            P("dp"),
            P("dp", "tensor"),
            P("dp", None),
            P("dp", "tensor"),
            P("dp"),
            P("dp", "tensor"),
            P("dp", "tensor"),
            P("dp", "tensor"),
        ),
        check_vma=False,
    )
```

```python
import functools

import jax
import jax.numpy as jnp
from jax import lax
from jax.experimental import pallas as pl
from jax.experimental.pallas import tpu as pltpu
from jax.sharding import PartitionSpec as P

HEAD = 128
WINDOW = 1024
BLOCK = 256
SPANS = WINDOW // BLOCK + 1

epsilon = 1e-06
negative = -1e30
low_type = jnp.bfloat16


def matmul(left, right):
    return jnp.dot(left, right, preferred_element_type=jnp.float32)


def times_transposed(left, right):
    return lax.dot_general(
        left, right, (((1,), (1,)), ((), ())), preferred_element_type=jnp.float32
    )


def outer_sum(left, right):
    return lax.dot_general(
        left, right, (((0,), (0,)), ((), ())), preferred_element_type=jnp.float32
    )


def flip(value, axis, bit):
    count = lax.axis_size(axis)
    return lax.ppermute(value, axis, [(i, i ^ bit) for i in range(count)])


def shift(value, step):
    count = lax.axis_size("dp")
    return lax.ppermute(value, "dp", [(i, (i + step) % count) for i in range(count)])


def gather_tensor(value):
    over = flip(value, "tensor", 2)
    return [value, flip(value, "tensor", 1), over, flip(over, "tensor", 1)]


def bit_of(index, bit):
    return (index >> bit) & 1


def pick(value, axis, index):
    return lax.dynamic_index_in_dim(value, index, axis, keepdims=False)


def reduce_weight_plain(pairs, order, dp):
    count = lax.axis_size("dp")
    bits = sorted(order, reverse=True)
    lefts = []
    for left, _ in pairs:
        lefts.append(left.reshape(left.shape[0], *([2] * len(bits)), -1))
    rights = [right for _, right in pairs]
    size = lefts[0].shape[-1]
    width = rights[0].shape[1]
    pending = []

    def product(chosen, waiting):
        total = None
        for left, right in zip(chosen, rights):
            part = outer_sum(left.reshape(left.shape[0], -1), right)
            total = part if total is None else total + part
        for item in waiting:
            total = total + item.reshape(total.shape).astype(jnp.float32)
        return total

    for bit in order:
        place = bits.index(bit)
        mine = bit_of(dp, bit)
        away = product(
            [pick(left, place + 1, 1 - mine) for left in lefts],
            [pick(item, place, 1 - mine) for item in pending],
        ).astype(low_type)
        arrived = flip(away, "dp", 1 << bit)
        bits.remove(bit)
        lefts = [pick(left, place + 1, mine) for left in lefts]
        pending = [pick(item, place, mine) for item in pending]
        pending.append(arrived.reshape(*([2] * len(bits)), size, width))
    return product(lefts, pending)


vmem_limit = 16 * 2**20
log2e = 1.4426950408889634
whole_vmem = pl.BlockSpec(memory_space=pltpu.VMEM)
whole_smem = pl.BlockSpec(memory_space=pltpu.SMEM)


def after(value, *others):
    return lax.optimization_barrier((value, *others))[0]


def cost(flops, transcendentals, *arrays):
    total = 0
    for item in arrays:
        total += item.size * item.dtype.itemsize
    return pl.CostEstimate(
        flops=int(flops), transcendentals=int(transcendentals), bytes_accessed=int(total)
    )


def parameters(limit=vmem_limit):
    return pltpu.CompilerParams(vmem_limit_bytes=limit)


def shape_of(shape, dtype):
    return jax.ShapeDtypeStruct(shape, dtype)


def turn(values, cosine, sine):
    return values * cosine + pltpu.roll(values, HEAD // 2, 1) * sine


def slot_facts(here, lengths, u, count):
    dp = here[0]
    slot = here[1] ^ u
    number = dp + slot * count
    start = jnp.int32(0)
    end = jnp.int32(0)
    for n in range(lengths.shape[0]):
        end = end + lengths[n]
        start = jnp.where(end <= number, end, start)
    pairs = [
        (slot if k == 0 else jnp.where(dp >= k, slot, 0)) ^ here[1] for k in range(SPANS)
    ]
    return number - start, pairs


def angle_tables(block, side, frequency, rows):
    place = lax.broadcasted_iota(jnp.int32, (rows, HEAD), 0) ^ (side * (BLOCK // 2))
    lane = lax.broadcasted_iota(jnp.int32, (rows, HEAD), 1)
    angle = (block * BLOCK + place).astype(jnp.float32) * frequency
    sine = jnp.sin(angle)
    return jnp.cos(angle), jnp.where(lane < HEAD // 2, -sine, sine)


def opening_kernel(
    here, lengths, x_ref, gain_ref, weight_ref, frequency_ref, normed_ref, keyval_ref, *, count
):
    x = x_ref[...].astype(jnp.float32)
    factor = lax.rsqrt(jnp.mean(x * x, axis=-1, keepdims=True) + epsilon)
    normed = (x * factor * gain_ref[...]).astype(low_type)
    normed_ref[...] = normed
    keyval = matmul(normed, weight_ref[...])
    block, _ = slot_facts(here, lengths, 0, count)
    cosine, sine = angle_tables(block, here[2], frequency_ref[...], x.shape[0])
    keyval_ref[:, :HEAD] = turn(keyval[:, :HEAD], cosine, sine).astype(low_type)
    keyval_ref[:, HEAD:] = keyval[:, HEAD:].astype(low_type)


def opening(here, lengths, x, gain, weight, frequency, count):
    outs = (
        shape_of(x.shape, low_type),
        shape_of((x.shape[0], weight.shape[1]), low_type),
    )
    return pl.pallas_call(
        functools.partial(opening_kernel, count=count),
        out_shape=outs,
        in_specs=[whole_smem] * 2 + [whole_vmem] * 4,
        out_specs=(whole_vmem, whole_vmem),
        compiler_params=parameters(),
        cost_estimate=cost(2 * x.size * weight.shape[1], x.shape[0], x, weight, *outs),
        name="opening",
    )(here, lengths, x, gain.reshape(1, -1), weight, frequency)


def tables_kernel(here, lengths, frequency_ref, normed_ref, cosine_ref, sine_ref, *, count):
    del normed_ref
    for u in range(2):
        block, _ = slot_facts(here, lengths, u, count)
        cosine, sine = angle_tables(block, here[2], frequency_ref[...], BLOCK)
        cosine_ref[u] = cosine
        sine_ref[u] = sine


def tables(here, lengths, frequency, earlier, count):
    out = shape_of((2, BLOCK, HEAD), jnp.float32)
    return pl.pallas_call(
        functools.partial(tables_kernel, count=count),
        out_shape=(out, out),
        in_specs=[whole_smem] * 2 + [whole_vmem, pl.BlockSpec(memory_space=pl.ANY)],
        out_specs=(whole_vmem, whole_vmem),
        compiler_params=parameters(),
        cost_estimate=cost(100 * out.size, 0, out, out),
        name="tables",
    )(here, lengths, frequency, earlier)


def project_kernel(normed_a, normed_b, weight_ref, cosine_ref, sine_ref, query_ref, *, u):
    normed = jnp.concatenate([normed_a[...], normed_b[...]], axis=0)
    raw = matmul(normed, weight_ref[...])
    for head in range(raw.shape[1] // HEAD):
        at = slice(head * HEAD, (head + 1) * HEAD)
        query_ref[:, at] = turn(raw[:, at], cosine_ref[u], sine_ref[u]).astype(low_type)


def project(normed, weight, cosine, sine, u):
    rows, width = normed[0].shape
    columns = weight.shape[1]
    out = shape_of((2 * rows, columns), low_type)
    return pl.pallas_call(
        functools.partial(project_kernel, u=u),
        out_shape=out,
        in_specs=[whole_vmem] * 5,
        out_specs=whole_vmem,
        compiler_params=parameters(),
        cost_estimate=cost(4 * rows * width * columns, 0, *normed, weight, out),
        name="project",
    )(*normed, weight, cosine, sine)


def stack_kernel(*refs):
    *parts, out_ref = refs
    for k, part in enumerate(parts):
        out_ref[k] = part[...]


def stack(parts):
    out = shape_of((len(parts), *parts[0].shape), parts[0].dtype)
    return pl.pallas_call(
        stack_kernel,
        out_shape=out,
        in_specs=[whole_vmem] * len(parts),
        out_specs=whole_vmem,
        compiler_params=parameters(),
        cost_estimate=cost(0, 0, out, out),
        name="stack",
    )(*parts)


def fill_window(pairs, keyvals, keys, values):
    half = BLOCK // 2
    for k in range(SPANS):
        for side in range(2):
            block = keyvals[side][k, pairs[k]]
            at = k * BLOCK + side * half
            keys[at : at + half, :] = block[:, :HEAD]
            values[at : at + half, :] = block[:, HEAD:]


def window_masks(block, side):
    swap = side * (BLOCK // 2)
    keys = lax.broadcasted_iota(jnp.int32, (BLOCK, BLOCK), 0) ^ swap
    rows = lax.broadcasted_iota(jnp.int32, (BLOCK, BLOCK), 1) ^ swap
    beyond = jnp.where(block >= SPANS - 1, 0, BLOCK)
    return keys <= rows, keys > rows + beyond


def masked(scores, k, masks, block):
    if k == 0:
        return jnp.where(masks[0], scores, negative)
    if k == SPANS - 1:
        return jnp.where(masks[1], scores, negative)
    return scores + jnp.where(block >= k, 0.0, negative)


def attend_kernel(
    here,
    lengths,
    query_ref,
    output_weight,
    keyval_0,
    keyval_1,
    even_ref,
    odd_ref,
    attended_ref,
    log_ref,
    keys,
    values,
    *,
    heads,
    u,
    count,
):
    block, pairs = slot_facts(here, lengths, u, count)
    fill_window(pairs, (keyval_0, keyval_1), keys, values)
    masks = window_masks(block, here[2])
    values_turned = values[...].T
    factor = HEAD ** (-0.5) * log2e
    for head in range(heads):
        at = slice(head * HEAD, (head + 1) * HEAD)
        query = query_ref[:, at]
        scores = []
        for k in range(SPANS):
            part = times_transposed(keys[k * BLOCK : (k + 1) * BLOCK, :], query) * factor
            scores.append(masked(part, k, masks, block))
        peak = jnp.max(scores[0], axis=0, keepdims=True)
        for part in scores[1:]:
            peak = jnp.maximum(peak, jnp.max(part, axis=0, keepdims=True))
        exponents = [jnp.exp2(part - peak) for part in scores]
        total = jnp.sum(exponents[0], axis=0, keepdims=True)
        for part in exponents[1:]:
            total = total + jnp.sum(part, axis=0, keepdims=True)
        inverse = 1.0 / total
        log_ref[head : head + 1, :] = peak + jnp.log(total) * log2e
        soft = jnp.concatenate([(part * inverse).astype(low_type) for part in exponents], axis=0)
        attended_ref[:, at] = matmul(values_turned, soft).T.astype(low_type)
    part = times_transposed(attended_ref[...], output_weight[...]).astype(low_type)
    even_ref[...] = part[: BLOCK // 2]
    odd_ref[...] = part[BLOCK // 2 :]


def attend(here, lengths, query, output_weight, keyvals, u, count):
    width, columns = output_weight.shape
    heads = columns // HEAD
    outs = (
        shape_of((BLOCK // 2, width), low_type),
        shape_of((BLOCK // 2, width), low_type),
        shape_of((BLOCK, columns), low_type),
        shape_of((8, BLOCK), jnp.float32),
    )
    flops = 2 * BLOCK * width * columns + 4 * BLOCK * SPANS * BLOCK * columns
    return pl.pallas_call(
        functools.partial(attend_kernel, heads=heads, u=u, count=count),
        out_shape=outs,
        in_specs=[whole_smem] * 2 + [whole_vmem] * 4,
        out_specs=(whole_vmem,) * 4,
        scratch_shapes=[pltpu.VMEM((SPANS * BLOCK, HEAD), low_type)] * 2,
        compiler_params=parameters(),
        cost_estimate=cost(
            flops, heads * SPANS * BLOCK * BLOCK, output_weight, *keyvals, *outs
        ),
        name="attend",
    )(here, lengths, query, output_weight, *keyvals)


def retreat_kernel(
    here,
    lengths,
    grad_a,
    grad_b,
    query_weight,
    output_weight,
    keyval_0,
    keyval_1,
    cosine_ref,
    sine_ref,
    query_ref,
    attended_ref,
    log_ref,
    *rest,
    heads,
    closing,
    u,
    count,
):
    block, pairs = slot_facts(here, lengths, u, count)
    if closing:
        other_keys, other_values = rest[:2]
        rest = rest[2:]
        even_ref, odd_ref, grad_query_ref, keep_0, keep_2, away = rest[:6]
        rest = rest[6:]
    else:
        even_ref, odd_ref, grad_query_ref, grad_keys, grad_values = rest[:5]
        rest = rest[5:]
    keys, values = rest[:2]
    if closing:
        grad_keys, grad_values = rest[2:4]
    fill_window(pairs, (keyval_0, keyval_1), keys, values)
    masks = window_masks(block, here[2])
    grad = jnp.concatenate([grad_a[...], grad_b[...]], axis=0)
    grad_attended = matmul(grad, output_weight[...]).astype(low_type)
    keys_turned = keys[...].T
    scale = HEAD ** (-0.5)
    factor = scale * log2e
    for head in range(heads):
        at = slice(head * HEAD, (head + 1) * HEAD)
        query = query_ref[:, at]
        grad_head = grad_attended[:, at]
        inner = jnp.sum(
            (grad_head.astype(jnp.float32) * attended_ref[:, at].astype(jnp.float32)).T,
            axis=0,
            keepdims=True,
        )
        log_row = log_ref[head : head + 1, :]
        grad_query = None
        for k in range(SPANS):
            span = slice(k * BLOCK, (k + 1) * BLOCK)
            part = times_transposed(keys[span, :], query) * factor
            soft = jnp.exp2(masked(part, k, masks, block) - log_row)
            grad_soft = times_transposed(values[span, :], grad_head)
            grad_scores = (soft * (grad_soft - inner)).astype(low_type)
            grad_key = matmul(grad_scores, query)
            grad_value = matmul(soft.astype(low_type), grad_head)
            if head == 0:
                grad_keys[span, :] = grad_key
                grad_values[span, :] = grad_value
            else:
                grad_keys[span, :] += grad_key
                grad_values[span, :] += grad_value
            step = matmul(keys_turned[:, span], grad_scores)
            grad_query = step if grad_query is None else grad_query + step
        grad_query_ref[:, at] = turn(
            grad_query.T * scale, cosine_ref[u], -sine_ref[u]
        ).astype(low_type)
    part = times_transposed(grad_query_ref[...], query_weight[...]).astype(low_type)
    even_ref[...] = part[: BLOCK // 2]
    odd_ref[...] = part[BLOCK // 2 :]
    if closing:
        _, other_pairs = slot_facts(here, lengths, 1 - u, count)
        half = BLOCK // 2
        for k in range(SPANS):
            for pair in range(2):
                mine = jnp.where(pairs[k] == pair, 1.0, 0.0)
                other = jnp.where(other_pairs[k] == pair, 1.0, 0.0)
                for side in range(2):
                    span = slice(k * BLOCK + side * half, k * BLOCK + (side + 1) * half)
                    key = (grad_keys[span, :] * mine + other_keys[span, :] * other) * scale
                    value = grad_values[span, :] * mine + other_values[span, :] * other
                    if side == 1:
                        away[pair, k, :, :HEAD] = key.astype(low_type)
                        away[pair, k, :, HEAD:] = value.astype(low_type)
                    else:
                        keep = keep_2 if pair else keep_0
                        keep[k, :, :HEAD] = key
                        keep[k, :, HEAD:] = value


def retreat(
    here,
    lengths,
    grads,
    query_weight,
    output_weight,
    keyvals,
    cosine,
    sine,
    query,
    attended,
    logs,
    other,
    u,
    count,
):
    rows, width = grads[0].shape
    columns = query_weight.shape[1]
    heads = columns // HEAD
    closing = other is not None
    outs = [
        shape_of((rows, width), low_type),
        shape_of((rows, width), low_type),
        shape_of((BLOCK, columns), low_type),
    ]
    window = (SPANS * BLOCK, HEAD)
    scratch = [pltpu.VMEM(window, low_type)] * 2
    operands = [
        here, lengths, *grads, query_weight, output_weight, *keyvals, cosine, sine, query,
        attended, logs,
    ]
    in_specs = [whole_smem] * 2 + [whole_vmem] * 11
    if closing:
        outs += [
            shape_of((SPANS, rows, 2 * HEAD), jnp.float32),
            shape_of((SPANS, rows, 2 * HEAD), jnp.float32),
            shape_of((2, SPANS, rows, 2 * HEAD), low_type),
        ]
        scratch += [pltpu.VMEM(window, jnp.float32)] * 2
        operands += other
        in_specs += [whole_vmem] * 2
    else:
        outs += [shape_of(window, jnp.float32)] * 2
    flops = 4 * BLOCK * width * columns + 10 * BLOCK * SPANS * BLOCK * columns
    return pl.pallas_call(
        functools.partial(retreat_kernel, heads=heads, closing=closing, u=u, count=count),
        out_shape=tuple(outs),
        in_specs=in_specs,
        out_specs=(whole_vmem,) * len(outs),
        scratch_shapes=scratch,
        compiler_params=parameters(20 * 2**20),
        cost_estimate=cost(
            flops, heads * SPANS * BLOCK * BLOCK, query_weight, output_weight, *keyvals, *outs
        ),
        name="retreat",
    )(*operands)


def return_kernel(here, lengths, *refs, count):
    *parts, frequency_ref, own_ref, out_ref = refs
    total = own_ref[0]
    for part in parts:
        total = total + part[...].astype(jnp.float32)
    block, _ = slot_facts(here, lengths, 0, count)
    cosine, sine = angle_tables(block, here[2], frequency_ref[...], total.shape[0])
    out_ref[:, :HEAD] = turn(total[:, :HEAD], cosine, -sine).astype(low_type)
    out_ref[:, HEAD:] = total[:, HEAD:].astype(low_type)


def return_keyval(here, lengths, parts, frequency, own, count):
    out = shape_of(parts[0].shape, low_type)
    return pl.pallas_call(
        functools.partial(return_kernel, count=count),
        out_shape=out,
        in_specs=[whole_smem] * 2 + [whole_vmem] * (len(parts) + 2),
        out_specs=whole_vmem,
        compiler_params=parameters(),
        cost_estimate=cost(0, out.size, out, *parts, own),
        name="return_keyval",
    )(here, lengths, *parts, frequency, own)


def column_tiles(columns, most=512):
    size = most
    while columns % size:
        size //= 2
    return [slice(at, at + size) for at in range(0, columns, size)]


def grad_product_kernel(*refs):
    *parts, weight_ref, out_ref = refs
    rows = jnp.concatenate([part[...] for part in parts], axis=0)
    for at in column_tiles(weight_ref.shape[1]):
        out_ref[:, at] = matmul(rows, weight_ref[:, at])


def grad_product(parts, weight):
    rows, width = parts[0].shape
    columns = weight.shape[1]
    out = shape_of((rows * len(parts), columns), jnp.float32)
    return pl.pallas_call(
        grad_product_kernel,
        out_shape=out,
        in_specs=[whole_vmem] * (len(parts) + 1),
        out_specs=whole_vmem,
        compiler_params=parameters(),
        cost_estimate=cost(2 * rows * len(parts) * width * columns, 0, *parts, weight, out),
        name="grad_product",
    )(*parts, weight)


def feed_kernel(*refs, count, grad_at, closing):
    parts = refs[:count]
    grad_ref, gate_ref, up_ref = refs[count : count + 3]
    hidden_ref, grad_gate_ref, grad_up_ref = refs[count + 3 : count + 6]
    rows = jnp.concatenate([part[...] for part in parts], axis=0)
    total_rows = rows.shape[0]
    for at in column_tiles(gate_ref.shape[1]):
        gate = matmul(rows, gate_ref[:, at])
        upper = matmul(rows, up_ref[:, at])
        grad = grad_ref[grad_at * total_rows : (grad_at + 1) * total_rows, at]
        activated, slope = gelu_parts(gate)
        hidden_ref[:, at] = (activated * upper).astype(low_type)
        grad_gate_ref[:, at] = (grad * upper * slope).astype(low_type)
        grad_up_ref[:, at] = (grad * activated).astype(low_type)
    if closing:
        even_ref, odd_ref = refs[count + 6 :]
        size = even_ref.shape[0]
        for at in column_tiles(gate_ref.shape[0]):
            total = times_transposed(grad_gate_ref[...], gate_ref[at, :]) + times_transposed(
                grad_up_ref[...], up_ref[at, :]
            )
            even_ref[:, at] = total[:size].astype(low_type)
            odd_ref[:, at] = total[size:].astype(low_type)


def feed(parts, grad, grad_at, gate_weight, up_weight, closing):
    rows, width = parts[0].shape
    columns = gate_weight.shape[1]
    total_rows = rows * len(parts)
    outs = [shape_of((total_rows, columns), low_type)] * 3
    if closing:
        outs += [shape_of((rows, width), low_type)] * 2
    flops = (8 if closing else 4) * total_rows * width * columns
    return pl.pallas_call(
        functools.partial(feed_kernel, count=len(parts), grad_at=grad_at, closing=closing),
        out_shape=tuple(outs),
        in_specs=[whole_vmem] * (len(parts) + 3),
        out_specs=(whole_vmem,) * len(outs),
        compiler_params=parameters(24 * 2**20),
        cost_estimate=cost(flops, total_rows * columns, gate_weight, up_weight, *outs, *outs[:1]),
        name="feed_back" if closing else "feed",
    )(*parts, grad, gate_weight, up_weight)


def weight_kernel(here, *refs, lefts, rights, known, free, waits, size):
    right = jnp.concatenate([ref[...] for ref in refs[lefts : lefts + rights]], axis=0)
    out_ref = refs[-1]
    every = sorted([*known, *free])

    def block_at(n, kept):
        total = jnp.int32(0)
        for place, bit in enumerate(kept):
            if bit in known:
                value = ((here[0] >> bit) & 1) ^ known[bit]
            else:
                value = jnp.int32((n >> free.index(bit)) & 1)
            total = total + (value << place)
        return pl.multiple_of(total * size, size)

    for n in range(1 << len(free)):
        span = pl.ds(block_at(n, every), size)
        left = jnp.concatenate([ref[:, span] for ref in refs[:lefts]], axis=0)
        total = matmul(left.T, right)
        for ref, kept in zip(refs[lefts + rights :], waits):
            total = total + ref[pl.ds(block_at(n, kept), size), :].astype(jnp.float32)
        out_ref[n * size : (n + 1) * size, :] = total.astype(out_ref.dtype)


def weight_blocks(here, lefts, rights, fixed, free, waiting, size, dtype):
    blocks = 1 << len(free)
    columns = rights[0].shape[1]
    tokens = sum(item.shape[0] for item in rights)
    out = shape_of((blocks * size, columns), dtype)
    arrays = [item for item, _ in waiting]
    return pl.pallas_call(
        functools.partial(
            weight_kernel,
            lefts=len(lefts),
            rights=len(rights),
            known=dict(fixed),
            free=list(free),
            waits=[kept for _, kept in waiting],
            size=size,
        ),
        out_shape=out,
        in_specs=[whole_smem] + [whole_vmem] * (len(lefts) + len(rights) + len(arrays)),
        out_specs=whole_vmem,
        compiler_params=parameters(20 * 2**20),
        cost_estimate=cost(
            2 * tokens * blocks * size * columns, 0, out, *lefts, *rights, *arrays
        ),
        name="weight_blocks",
    )(here, *lefts, *rights, *arrays)


class WeightSum:
    def __init__(self, here, lefts, rights, order, fixed=()):
        self.here = here
        self.lefts = lefts
        self.rights = rights
        self.bits = list(order)
        self.known = [(bit, 0) for bit in fixed]
        self.waiting = []
        self.size = lefts[0].shape[1] // lax.axis_size("dp")
        self.plain = self.size % HEAD != 0
        self.fixed = fixed
        self.last = lefts[0]

    def send(self):
        bit = self.bits.pop(0)
        away = weight_blocks(
            self.here,
            self.lefts,
            self.rights,
            [*self.known, (bit, 1)],
            self.bits,
            self.waiting,
            self.size,
            low_type,
        )
        self.known.append((bit, 0))
        return away, bit

    def receive(self, away, bit):
        self.last = away
        self.waiting.append((flip(away, "dp", 1 << bit), list(self.bits)))

    def step(self):
        if not self.plain:
            self.receive(*self.send())

    def finish(self):
        if not self.plain:
            return weight_blocks(
                self.here,
                self.lefts,
                self.rights,
                self.known,
                [],
                self.waiting,
                self.size,
                jnp.float32,
            )
        dp = lax.axis_index("dp")
        left = jnp.concatenate(self.lefts)
        for bit in self.fixed:
            left = left.reshape(left.shape[0], -1, 2, self.size << bit)
            left = pick(left, 2, bit_of(dp, bit)).reshape(left.shape[0], -1)
        return reduce_weight_plain(
            [(left, jnp.concatenate(self.rights))], self.bits, dp
        )


def gelu_parts(gate):
    root = 0.7978845608028654
    square = gate * gate
    curve = jnp.tanh(root * gate * (1.0 + 0.044715 * square))
    half = 0.5 * (1.0 + curve)
    slope = half + 0.5 * gate * (1.0 - curve * curve) * root * (1.0 + 3 * 0.044715 * square)
    return gate * half, slope


def norm_back(grad, scaled, factor, gain):
    grad_scaled = grad * gain
    inner = jnp.mean(grad_scaled * scaled, axis=-1, keepdims=True)
    return factor * (grad_scaled - scaled * inner)


def to_float(value):
    return value.astype(jnp.float32)


def per_device(
    block_input,
    cotangent,
    sequence_blocks,
    gain_attention,
    query_weight,
    keyval_weight,
    output_weight,
    gain_feedforward,
    gate_weight,
    up_weight,
    down_weight,
):
    count = lax.axis_size("dp")
    bits = count.bit_length() - 1
    dp = lax.axis_index("dp")
    rank = lax.axis_index("tensor")
    rows = block_input.shape[0]
    width = block_input.shape[1]
    top = bits - 1
    here = jnp.stack([dp, rank >> 1, rank & 1, rank]).astype(jnp.int32)
    lengths = sequence_blocks
    lane = jnp.arange(HEAD, dtype=jnp.float32) % (HEAD // 2)
    frequency = (10000.0 ** (-lane * 2.0 / HEAD))[None, :]

    def core(value):
        return flip(value, "tensor", 1)

    def over(value):
        return flip(value, "tensor", 2)

    own_normed, own_keyval = opening(
        here, lengths, block_input, gain_attention, keyval_weight, frequency, count
    )
    keyval_over = flip(own_keyval, "tensor", 2)
    near = stack([own_keyval, keyval_over])
    cosine, sine = tables(here, lengths, frequency, own_keyval, count)
    normed = [own_normed, core(own_normed), over(after(own_normed, near))]
    normed.append(core(normed[2]))
    spread = stack([near] + [shift(near, k) for k in range(1, SPANS)])
    across = flip(spread, "tensor", 1)
    keyvals = [spread, across]
    query_0 = project(normed[:2], query_weight, cosine, sine, 0)
    query_1 = project(normed[2:], query_weight, cosine, sine, 1)

    late_cotangent = after(cotangent, spread)
    cotangents = gather_tensor(late_cotangent)
    cotangent_far = flip(late_cotangent, "dp", 1 << top)

    even_1, odd_1, attended_1, logs_1 = attend(
        here, lengths, query_1, output_weight, keyvals, 1, count
    )
    even_0, odd_0, attended_0, logs_0 = attend(
        here, lengths, after(query_0, even_1), output_weight, keyvals, 0, count
    )

    def scatter(even_front, odd_front, even_back, odd_back):
        far = to_float(even_back) + to_float(flip(odd_back, "tensor", 1))
        near = to_float(even_front) + to_float(flip(odd_front, "tensor", 1))
        return near + to_float(flip(far.astype(low_type), "tensor", 2))

    own_input = to_float(block_input)
    own_hidden = own_input + scatter(even_0, odd_0, even_1, odd_1)
    factor_two = lax.rsqrt(jnp.mean(own_hidden * own_hidden, axis=-1, keepdims=True) + epsilon)
    scaled_two = own_hidden * factor_two
    own_normed_two = (scaled_two * gain_feedforward).astype(low_type)
    grad_hidden = grad_product(
        [after(cotangents[0], even_0), *cotangents[1:]], down_weight
    )
    normed_two = gather_tensor(own_normed_two)
    far_two = flip(own_normed_two, "dp", 1 << top)

    hidden_0, grad_gate_0, grad_up_0, back_even_0, back_odd_0 = feed(
        normed_two[:2], grad_hidden, 0, gate_weight, up_weight, True
    )
    hidden_1, grad_gate_1, grad_up_1, back_even_1, back_odd_1 = feed(
        [after(normed_two[2], back_even_0), normed_two[3]], grad_hidden, 1, gate_weight, up_weight, True
    )
    normed_two_far = gather_tensor(after(far_two, normed_two[2]))
    cotangents_far = gather_tensor(after(cotangent_far, own_normed_two))
    own_grad_two = scatter(back_even_0, back_odd_0, back_even_1, back_odd_1)
    own_grad_hidden = to_float(cotangent) + norm_back(
        own_grad_two, scaled_two, factor_two, gain_feedforward
    )
    own_grad_low = own_grad_hidden.astype(low_type)
    grad_attention = gather_tensor(own_grad_low)
    grad_hidden_far = grad_product(
        [after(cotangents_far[0], back_even_1), *cotangents_far[1:]], down_weight
    )
    hidden_far, grad_gate_far, grad_up_far = feed(
        normed_two_far, grad_hidden_far, 0, gate_weight, up_weight, False
    )

    both_normed_two = [*normed_two, *normed_two_far]
    low_order = list(range(top))
    down_sum = WeightSum(
        here,
        [*cotangents, *cotangents_far],
        [hidden_0, hidden_1, hidden_far],
        low_order[::-1],
        (top,),
    )
    gate_sum = WeightSum(
        here, both_normed_two, [grad_gate_0, grad_gate_1, grad_gate_far], low_order, (top,)
    )
    up_sum = WeightSum(
        here, both_normed_two, [grad_up_0, grad_up_1, grad_up_far], low_order, (top,)
    )
    sums = (gate_sum, down_sum, up_sum)
    for item in sums:
        item.step()

    back_even_0, back_odd_0, grad_query_0, window_keys, window_values = retreat(
        here,
        lengths,
        grad_attention[:2],
        query_weight,
        output_weight,
        keyvals,
        cosine,
        sine,
        query_0,
        attended_0,
        logs_0,
        None,
        0,
        count,
    )
    back_even_1, back_odd_1, grad_query_1, keep_0, keep_2, away = retreat(
        here,
        lengths,
        grad_attention[2:],
        query_weight,
        output_weight,
        keyvals,
        cosine,
        sine,
        query_1,
        attended_1,
        logs_1,
        [window_keys, window_values],
        1,
        count,
    )
    arrived = flip(away, "tensor", 1)
    far_returns = (keep_2 + to_float(arrived[1])).astype(low_type)
    own_returns = keep_0 + to_float(arrived[0]) + to_float(flip(far_returns, "tensor", 2))
    back = [shift(own_returns[k].astype(low_type), -k) for k in range(1, SPANS)]
    own_grad_keyval = return_keyval(here, lengths, back, frequency, own_returns[:1], count)

    for item in sums:
        for _ in range(len(item.bits)):
            item.step()
    grad_down = down_sum.finish()
    grad_gate_weight = gate_sum.finish()
    grad_up_weight = up_sum.finish()

    query_sum = WeightSum(here, normed, [grad_query_0, grad_query_1], [*low_order, top])
    output_sum = WeightSum(
        here, grad_attention, [attended_0, attended_1], [*low_order[::-1], top]
    )
    for _ in range(bits):
        query_sum.step()
    for _ in range(bits):
        output_sum.step()
    grad_query_weight = query_sum.finish()
    grad_output_weight = output_sum.finish()

    own_grad_one = scatter(back_even_0, back_odd_0, back_even_1, back_odd_1) + times_transposed(
        own_grad_keyval, keyval_weight
    )
    factor_one = lax.rsqrt(jnp.mean(own_input * own_input, axis=-1, keepdims=True) + epsilon)
    grad_rows = own_grad_hidden + norm_back(
        own_grad_one, own_input * factor_one, factor_one, gain_attention
    )

    quarter = 2 * HEAD // 4
    grad_keyval = jnp.concatenate(gather_tensor(own_grad_keyval))
    part = lax.dynamic_slice_in_dim(grad_keyval, rank * quarter, quarter, 1)
    keyval_sum = WeightSum(here, normed, [part], [*low_order, top])
    for _ in range(bits):
        keyval_sum.step()
    pieces = jnp.stack(gather_tensor(keyval_sum.finish().T))
    pieces = [pick(pieces, 0, rank ^ g).reshape(quarter, -1) for g in range(4)]
    grad_keyval_weight = jnp.concatenate(pieces).T

    down_front = times_transposed(hidden_0, down_weight).astype(low_type)
    down_back = times_transposed(hidden_1, down_weight).astype(low_type)
    block_output = (
        own_hidden
        + scatter(down_front[:rows], down_front[rows:], down_back[:rows], down_back[rows:])
    ).astype(low_type)

    size = width // count

    def own_block(value):
        return lax.dynamic_slice_in_dim(value, dp * size, size, 0)

    def sum_tensor(value):
        value = value + flip(value, "tensor", 1)
        return value + flip(value, "tensor", 2)

    gain_two = sum_tensor(
        jnp.sum(to_float(own_block(gate_weight)) * grad_gate_weight, axis=1)
        + jnp.sum(to_float(own_block(up_weight)) * grad_up_weight, axis=1)
    ) / own_block(gain_feedforward)
    gain_one = (
        sum_tensor(jnp.sum(to_float(own_block(query_weight)) * grad_query_weight, axis=1))
        + jnp.sum(to_float(own_block(keyval_weight)) * grad_keyval_weight, axis=1)
    ) / own_block(gain_attention)
    return (
        block_output,
        grad_rows,
        gain_one,
        grad_query_weight,
        grad_keyval_weight,
        grad_output_weight,
        gain_two,
        grad_gate_weight,
        grad_up_weight,
        grad_down,
    )


def solution(mesh):
    placed = (
        P(("dp", "tensor"), None),
        P(("dp", "tensor"), None),
        P(),
        P(),
        P(None, "tensor"),
        P(),
        P(None, "tensor"),
        P(),
        P(None, "tensor"),
        P(None, "tensor"),
        P(None, "tensor"),
    )
    return jax.shard_map(
        per_device,
        mesh=mesh,
        in_specs=placed,
        out_specs=(
            P(("dp", "tensor"), None),
            P(("dp", "tensor"), None),
            P("dp"),
            P("dp", "tensor"),
            P("dp", None),
            P("dp", "tensor"),
            P("dp"),
            P("dp", "tensor"),
            P("dp", "tensor"),
            P("dp", "tensor"),
        ),
        check_vma=False,
    )
```

```python
import functools

import jax
import jax.numpy as jnp
from jax import lax
from jax.experimental import pallas as pl
from jax.experimental.pallas import tpu as pltpu
from jax.sharding import PartitionSpec as P

HEAD = 128
WINDOW = 1024
BLOCK = 256
SPANS = WINDOW // BLOCK + 1

epsilon = 1e-06
negative = -1e30
low_type = jnp.bfloat16


def matmul(left, right):
    return jnp.dot(left, right, preferred_element_type=jnp.float32)


def times_transposed(left, right):
    return lax.dot_general(
        left, right, (((1,), (1,)), ((), ())), preferred_element_type=jnp.float32
    )


def outer_sum(left, right):
    return lax.dot_general(
        left, right, (((0,), (0,)), ((), ())), preferred_element_type=jnp.float32
    )


def flip(value, axis, bit):
    count = lax.axis_size(axis)
    return lax.ppermute(value, axis, [(i, i ^ bit) for i in range(count)])


def shift(value, step):
    count = lax.axis_size("dp")
    return lax.ppermute(value, "dp", [(i, (i + step) % count) for i in range(count)])


def gather_tensor(value):
    over = flip(value, "tensor", 2)
    return [value, flip(value, "tensor", 1), over, flip(over, "tensor", 1)]


def bit_of(index, bit):
    return (index >> bit) & 1


def pick(value, axis, index):
    return lax.dynamic_index_in_dim(value, index, axis, keepdims=False)


def reduce_weight_plain(pairs, order, dp):
    count = lax.axis_size("dp")
    bits = sorted(order, reverse=True)
    lefts = []
    for left, _ in pairs:
        lefts.append(left.reshape(left.shape[0], *([2] * len(bits)), -1))
    rights = [right for _, right in pairs]
    size = lefts[0].shape[-1]
    width = rights[0].shape[1]
    pending = []

    def product(chosen, waiting):
        total = None
        for left, right in zip(chosen, rights):
            part = outer_sum(left.reshape(left.shape[0], -1), right)
            total = part if total is None else total + part
        for item in waiting:
            total = total + item.reshape(total.shape).astype(jnp.float32)
        return total

    for bit in order:
        place = bits.index(bit)
        mine = bit_of(dp, bit)
        away = product(
            [pick(left, place + 1, 1 - mine) for left in lefts],
            [pick(item, place, 1 - mine) for item in pending],
        ).astype(low_type)
        arrived = flip(away, "dp", 1 << bit)
        bits.remove(bit)
        lefts = [pick(left, place + 1, mine) for left in lefts]
        pending = [pick(item, place, mine) for item in pending]
        pending.append(arrived.reshape(*([2] * len(bits)), size, width))
    return product(lefts, pending)


vmem_limit = 16 * 2**20
log2e = 1.4426950408889634
whole_vmem = pl.BlockSpec(memory_space=pltpu.VMEM)
whole_smem = pl.BlockSpec(memory_space=pltpu.SMEM)


def after(value, *others):
    return lax.optimization_barrier((value, *others))[0]


def cost(flops, transcendentals, *arrays):
    total = 0
    for item in arrays:
        total += item.size * item.dtype.itemsize
    return pl.CostEstimate(
        flops=int(flops), transcendentals=int(transcendentals), bytes_accessed=int(total)
    )


def parameters(limit=vmem_limit):
    return pltpu.CompilerParams(vmem_limit_bytes=limit)


def shape_of(shape, dtype):
    return jax.ShapeDtypeStruct(shape, dtype)


def turn(values, cosine, sine):
    return values * cosine + pltpu.roll(values, HEAD // 2, 1) * sine


def slot_facts(here, lengths, u, count):
    dp = here[0]
    slot = here[1] ^ u
    number = dp + slot * count
    start = jnp.int32(0)
    end = jnp.int32(0)
    for n in range(lengths.shape[0]):
        end = end + lengths[n]
        start = jnp.where(end <= number, end, start)
    pairs = [
        (slot if k == 0 else jnp.where(dp >= k, slot, 0)) ^ here[1] for k in range(SPANS)
    ]
    return number - start, pairs


def angle_tables(block, side, frequency, rows):
    place = lax.broadcasted_iota(jnp.int32, (rows, HEAD), 0) ^ (side * (BLOCK // 2))
    lane = lax.broadcasted_iota(jnp.int32, (rows, HEAD), 1)
    angle = (block * BLOCK + place).astype(jnp.float32) * frequency
    sine = jnp.sin(angle)
    return jnp.cos(angle), jnp.where(lane < HEAD // 2, -sine, sine)


def opening_kernel(
    here, lengths, x_ref, gain_ref, weight_ref, frequency_ref, normed_ref, keyval_ref, *, count
):
    x = x_ref[...].astype(jnp.float32)
    factor = lax.rsqrt(jnp.mean(x * x, axis=-1, keepdims=True) + epsilon)
    normed = (x * factor * gain_ref[...]).astype(low_type)
    normed_ref[...] = normed
    keyval = matmul(normed, weight_ref[...])
    block, _ = slot_facts(here, lengths, 0, count)
    cosine, sine = angle_tables(block, here[2], frequency_ref[...], x.shape[0])
    keyval_ref[:, :HEAD] = turn(keyval[:, :HEAD], cosine, sine).astype(low_type)
    keyval_ref[:, HEAD:] = keyval[:, HEAD:].astype(low_type)


def opening(here, lengths, x, gain, weight, frequency, count):
    outs = (
        shape_of(x.shape, low_type),
        shape_of((x.shape[0], weight.shape[1]), low_type),
    )
    return pl.pallas_call(
        functools.partial(opening_kernel, count=count),
        out_shape=outs,
        in_specs=[whole_smem] * 2 + [whole_vmem] * 4,
        out_specs=(whole_vmem, whole_vmem),
        compiler_params=parameters(),
        cost_estimate=cost(2 * x.size * weight.shape[1], x.shape[0], x, weight, *outs),
        name="opening",
    )(here, lengths, x, gain.reshape(1, -1), weight, frequency)


def tables_kernel(here, lengths, frequency_ref, normed_ref, cosine_ref, sine_ref, *, count):
    del normed_ref
    for u in range(2):
        block, _ = slot_facts(here, lengths, u, count)
        cosine, sine = angle_tables(block, here[2], frequency_ref[...], BLOCK)
        cosine_ref[u] = cosine
        sine_ref[u] = sine


def tables(here, lengths, frequency, earlier, count):
    out = shape_of((2, BLOCK, HEAD), jnp.float32)
    return pl.pallas_call(
        functools.partial(tables_kernel, count=count),
        out_shape=(out, out),
        in_specs=[whole_smem] * 2 + [whole_vmem, pl.BlockSpec(memory_space=pl.ANY)],
        out_specs=(whole_vmem, whole_vmem),
        compiler_params=parameters(),
        cost_estimate=cost(100 * out.size, 0, out, out),
        name="tables",
    )(here, lengths, frequency, earlier)


def project_kernel(normed_a, normed_b, weight_ref, cosine_ref, sine_ref, query_ref, *, u):
    normed = jnp.concatenate([normed_a[...], normed_b[...]], axis=0)
    raw = matmul(normed, weight_ref[...])
    for head in range(raw.shape[1] // HEAD):
        at = slice(head * HEAD, (head + 1) * HEAD)
        query_ref[:, at] = turn(raw[:, at], cosine_ref[u], sine_ref[u]).astype(low_type)


def project(normed, weight, cosine, sine, u):
    rows, width = normed[0].shape
    columns = weight.shape[1]
    out = shape_of((2 * rows, columns), low_type)
    return pl.pallas_call(
        functools.partial(project_kernel, u=u),
        out_shape=out,
        in_specs=[whole_vmem] * 5,
        out_specs=whole_vmem,
        compiler_params=parameters(),
        cost_estimate=cost(4 * rows * width * columns, 0, *normed, weight, out),
        name="project",
    )(*normed, weight, cosine, sine)


def stack_kernel(*refs):
    *parts, out_ref = refs
    for k, part in enumerate(parts):
        out_ref[k] = part[...]


def stack(parts):
    out = shape_of((len(parts), *parts[0].shape), parts[0].dtype)
    return pl.pallas_call(
        stack_kernel,
        out_shape=out,
        in_specs=[whole_vmem] * len(parts),
        out_specs=whole_vmem,
        compiler_params=parameters(),
        cost_estimate=cost(0, 0, out, out),
        name="stack",
    )(*parts)


def fill_window(pairs, keyvals, keys, values):
    half = BLOCK // 2
    for k in range(SPANS):
        for side in range(2):
            block = keyvals[side][k, pairs[k]]
            at = k * BLOCK + side * half
            keys[at : at + half, :] = block[:, :HEAD]
            values[at : at + half, :] = block[:, HEAD:]


def window_masks(block, side):
    swap = side * (BLOCK // 2)
    keys = lax.broadcasted_iota(jnp.int32, (BLOCK, BLOCK), 0) ^ swap
    rows = lax.broadcasted_iota(jnp.int32, (BLOCK, BLOCK), 1) ^ swap
    beyond = jnp.where(block >= SPANS - 1, 0, BLOCK)
    return keys <= rows, keys > rows + beyond


def masked(scores, k, masks, block):
    if k == 0:
        return jnp.where(masks[0], scores, negative)
    if k == SPANS - 1:
        return jnp.where(masks[1], scores, negative)
    return scores + jnp.where(block >= k, 0.0, negative)


def attend_kernel(
    here,
    lengths,
    query_ref,
    output_weight,
    keyval_0,
    keyval_1,
    even_ref,
    odd_ref,
    attended_ref,
    log_ref,
    keys,
    values,
    *,
    heads,
    u,
    count,
):
    block, pairs = slot_facts(here, lengths, u, count)
    fill_window(pairs, (keyval_0, keyval_1), keys, values)
    masks = window_masks(block, here[2])
    values_turned = values[...].T
    factor = HEAD ** (-0.5) * log2e
    for head in range(heads):
        at = slice(head * HEAD, (head + 1) * HEAD)
        query = query_ref[:, at]
        scores = []
        for k in range(SPANS):
            part = times_transposed(keys[k * BLOCK : (k + 1) * BLOCK, :], query) * factor
            scores.append(masked(part, k, masks, block))
        peak = jnp.max(scores[0], axis=0, keepdims=True)
        for part in scores[1:]:
            peak = jnp.maximum(peak, jnp.max(part, axis=0, keepdims=True))
        exponents = [jnp.exp2(part - peak) for part in scores]
        total = jnp.sum(exponents[0], axis=0, keepdims=True)
        for part in exponents[1:]:
            total = total + jnp.sum(part, axis=0, keepdims=True)
        inverse = 1.0 / total
        log_ref[head : head + 1, :] = peak + jnp.log(total) * log2e
        soft = jnp.concatenate([(part * inverse).astype(low_type) for part in exponents], axis=0)
        attended_ref[:, at] = matmul(values_turned, soft).T.astype(low_type)
    part = times_transposed(attended_ref[...], output_weight[...]).astype(low_type)
    even_ref[...] = part[: BLOCK // 2]
    odd_ref[...] = part[BLOCK // 2 :]


def attend(here, lengths, query, output_weight, keyvals, u, count):
    width, columns = output_weight.shape
    heads = columns // HEAD
    outs = (
        shape_of((BLOCK // 2, width), low_type),
        shape_of((BLOCK // 2, width), low_type),
        shape_of((BLOCK, columns), low_type),
        shape_of((8, BLOCK), jnp.float32),
    )
    flops = 2 * BLOCK * width * columns + 4 * BLOCK * SPANS * BLOCK * columns
    return pl.pallas_call(
        functools.partial(attend_kernel, heads=heads, u=u, count=count),
        out_shape=outs,
        in_specs=[whole_smem] * 2 + [whole_vmem] * 4,
        out_specs=(whole_vmem,) * 4,
        scratch_shapes=[pltpu.VMEM((SPANS * BLOCK, HEAD), low_type)] * 2,
        compiler_params=parameters(),
        cost_estimate=cost(
            flops, heads * SPANS * BLOCK * BLOCK, output_weight, *keyvals, *outs
        ),
        name="attend",
    )(here, lengths, query, output_weight, *keyvals)


def retreat_kernel(
    here,
    lengths,
    grad_a,
    grad_b,
    query_weight,
    output_weight,
    keyval_0,
    keyval_1,
    cosine_ref,
    sine_ref,
    query_ref,
    attended_ref,
    log_ref,
    *rest,
    heads,
    closing,
    u,
    count,
):
    block, pairs = slot_facts(here, lengths, u, count)
    if closing:
        other_keys, other_values = rest[:2]
        rest = rest[2:]
        even_ref, odd_ref, grad_query_ref, keep_0, keep_2, away = rest[:6]
        rest = rest[6:]
    else:
        even_ref, odd_ref, grad_query_ref, grad_keys, grad_values = rest[:5]
        rest = rest[5:]
    keys, values = rest[:2]
    if closing:
        grad_keys, grad_values = rest[2:4]
    fill_window(pairs, (keyval_0, keyval_1), keys, values)
    masks = window_masks(block, here[2])
    grad = jnp.concatenate([grad_a[...], grad_b[...]], axis=0)
    grad_attended = matmul(grad, output_weight[...]).astype(low_type)
    keys_turned = keys[...].T
    scale = HEAD ** (-0.5)
    factor = scale * log2e
    for head in range(heads):
        at = slice(head * HEAD, (head + 1) * HEAD)
        query = query_ref[:, at]
        grad_head = grad_attended[:, at]
        inner = jnp.sum(
            (grad_head.astype(jnp.float32) * attended_ref[:, at].astype(jnp.float32)).T,
            axis=0,
            keepdims=True,
        )
        log_row = log_ref[head : head + 1, :]
        grad_query = None
        for k in range(SPANS):
            span = slice(k * BLOCK, (k + 1) * BLOCK)
            part = times_transposed(keys[span, :], query) * factor
            soft = jnp.exp2(masked(part, k, masks, block) - log_row)
            grad_soft = times_transposed(values[span, :], grad_head)
            grad_scores = (soft * (grad_soft - inner)).astype(low_type)
            grad_key = matmul(grad_scores, query)
            grad_value = matmul(soft.astype(low_type), grad_head)
            if head == 0:
                grad_keys[span, :] = grad_key
                grad_values[span, :] = grad_value
            else:
                grad_keys[span, :] += grad_key
                grad_values[span, :] += grad_value
            step = matmul(keys_turned[:, span], grad_scores)
            grad_query = step if grad_query is None else grad_query + step
        grad_query_ref[:, at] = turn(
            grad_query.T * scale, cosine_ref[u], -sine_ref[u]
        ).astype(low_type)
    part = times_transposed(grad_query_ref[...], query_weight[...]).astype(low_type)
    even_ref[...] = part[: BLOCK // 2]
    odd_ref[...] = part[BLOCK // 2 :]
    if closing:
        _, other_pairs = slot_facts(here, lengths, 1 - u, count)
        half = BLOCK // 2
        for k in range(SPANS):
            for pair in range(2):
                mine = jnp.where(pairs[k] == pair, 1.0, 0.0)
                other = jnp.where(other_pairs[k] == pair, 1.0, 0.0)
                for side in range(2):
                    span = slice(k * BLOCK + side * half, k * BLOCK + (side + 1) * half)
                    key = (grad_keys[span, :] * mine + other_keys[span, :] * other) * scale
                    value = grad_values[span, :] * mine + other_values[span, :] * other
                    if side == 1:
                        away[pair, k, :, :HEAD] = key.astype(low_type)
                        away[pair, k, :, HEAD:] = value.astype(low_type)
                    else:
                        keep = keep_2 if pair else keep_0
                        keep[k, :, :HEAD] = key
                        keep[k, :, HEAD:] = value


def retreat(
    here,
    lengths,
    grads,
    query_weight,
    output_weight,
    keyvals,
    cosine,
    sine,
    query,
    attended,
    logs,
    other,
    u,
    count,
):
    rows, width = grads[0].shape
    columns = query_weight.shape[1]
    heads = columns // HEAD
    closing = other is not None
    outs = [
        shape_of((rows, width), low_type),
        shape_of((rows, width), low_type),
        shape_of((BLOCK, columns), low_type),
    ]
    window = (SPANS * BLOCK, HEAD)
    scratch = [pltpu.VMEM(window, low_type)] * 2
    operands = [
        here, lengths, *grads, query_weight, output_weight, *keyvals, cosine, sine, query,
        attended, logs,
    ]
    in_specs = [whole_smem] * 2 + [whole_vmem] * 11
    if closing:
        outs += [
            shape_of((SPANS, rows, 2 * HEAD), jnp.float32),
            shape_of((SPANS, rows, 2 * HEAD), jnp.float32),
            shape_of((2, SPANS, rows, 2 * HEAD), low_type),
        ]
        scratch += [pltpu.VMEM(window, jnp.float32)] * 2
        operands += other
        in_specs += [whole_vmem] * 2
    else:
        outs += [shape_of(window, jnp.float32)] * 2
    flops = 4 * BLOCK * width * columns + 10 * BLOCK * SPANS * BLOCK * columns
    return pl.pallas_call(
        functools.partial(retreat_kernel, heads=heads, closing=closing, u=u, count=count),
        out_shape=tuple(outs),
        in_specs=in_specs,
        out_specs=(whole_vmem,) * len(outs),
        scratch_shapes=scratch,
        compiler_params=parameters(20 * 2**20),
        cost_estimate=cost(
            flops, heads * SPANS * BLOCK * BLOCK, query_weight, output_weight, *keyvals, *outs
        ),
        name="retreat",
    )(*operands)


def return_kernel(here, lengths, *refs, count):
    *parts, frequency_ref, own_ref, out_ref = refs
    total = own_ref[0]
    for part in parts:
        total = total + part[...].astype(jnp.float32)
    block, _ = slot_facts(here, lengths, 0, count)
    cosine, sine = angle_tables(block, here[2], frequency_ref[...], total.shape[0])
    out_ref[:, :HEAD] = turn(total[:, :HEAD], cosine, -sine).astype(low_type)
    out_ref[:, HEAD:] = total[:, HEAD:].astype(low_type)


def return_keyval(here, lengths, parts, frequency, own, count):
    out = shape_of(parts[0].shape, low_type)
    return pl.pallas_call(
        functools.partial(return_kernel, count=count),
        out_shape=out,
        in_specs=[whole_smem] * 2 + [whole_vmem] * (len(parts) + 2),
        out_specs=whole_vmem,
        compiler_params=parameters(),
        cost_estimate=cost(0, out.size, out, *parts, own),
        name="return_keyval",
    )(here, lengths, *parts, frequency, own)


def column_tiles(columns, most=512):
    size = most
    while columns % size:
        size //= 2
    return [slice(at, at + size) for at in range(0, columns, size)]


def grad_product_kernel(*refs):
    *parts, weight_ref, out_ref = refs
    rows = jnp.concatenate([part[...] for part in parts], axis=0)
    for at in column_tiles(weight_ref.shape[1]):
        out_ref[:, at] = matmul(rows, weight_ref[:, at])


def grad_product(parts, weight):
    rows, width = parts[0].shape
    columns = weight.shape[1]
    out = shape_of((rows * len(parts), columns), jnp.float32)
    return pl.pallas_call(
        grad_product_kernel,
        out_shape=out,
        in_specs=[whole_vmem] * (len(parts) + 1),
        out_specs=whole_vmem,
        compiler_params=parameters(),
        cost_estimate=cost(2 * rows * len(parts) * width * columns, 0, *parts, weight, out),
        name="grad_product",
    )(*parts, weight)


def feed_kernel(*refs, count, grad_at, closing):
    parts = refs[:count]
    grad_ref, gate_ref, up_ref = refs[count : count + 3]
    hidden_ref, grad_gate_ref, grad_up_ref = refs[count + 3 : count + 6]
    rows = jnp.concatenate([part[...] for part in parts], axis=0)
    total_rows = rows.shape[0]
    for at in column_tiles(gate_ref.shape[1]):
        gate = matmul(rows, gate_ref[:, at])
        upper = matmul(rows, up_ref[:, at])
        grad = grad_ref[grad_at * total_rows : (grad_at + 1) * total_rows, at]
        activated, slope = gelu_parts(gate)
        hidden_ref[:, at] = (activated * upper).astype(low_type)
        grad_gate_ref[:, at] = (grad * upper * slope).astype(low_type)
        grad_up_ref[:, at] = (grad * activated).astype(low_type)
    if closing:
        even_ref, odd_ref = refs[count + 6 :]
        size = even_ref.shape[0]
        for at in column_tiles(gate_ref.shape[0]):
            total = times_transposed(grad_gate_ref[...], gate_ref[at, :]) + times_transposed(
                grad_up_ref[...], up_ref[at, :]
            )
            even_ref[:, at] = total[:size].astype(low_type)
            odd_ref[:, at] = total[size:].astype(low_type)


def feed(parts, grad, grad_at, gate_weight, up_weight, closing):
    rows, width = parts[0].shape
    columns = gate_weight.shape[1]
    total_rows = rows * len(parts)
    outs = [shape_of((total_rows, columns), low_type)] * 3
    if closing:
        outs += [shape_of((rows, width), low_type)] * 2
    flops = (8 if closing else 4) * total_rows * width * columns
    return pl.pallas_call(
        functools.partial(feed_kernel, count=len(parts), grad_at=grad_at, closing=closing),
        out_shape=tuple(outs),
        in_specs=[whole_vmem] * (len(parts) + 3),
        out_specs=(whole_vmem,) * len(outs),
        compiler_params=parameters(24 * 2**20),
        cost_estimate=cost(flops, total_rows * columns, gate_weight, up_weight, *outs, *outs[:1]),
        name="feed_back" if closing else "feed",
    )(*parts, grad, gate_weight, up_weight)


def weight_kernel(here, *refs, lefts, rights, known, free, waits, size):
    right = jnp.concatenate([ref[...] for ref in refs[lefts : lefts + rights]], axis=0)
    out_ref = refs[-1]
    every = sorted([*known, *free])

    def block_at(n, kept):
        total = jnp.int32(0)
        for place, bit in enumerate(kept):
            if bit in known:
                value = ((here[0] >> bit) & 1) ^ known[bit]
            else:
                value = jnp.int32((n >> free.index(bit)) & 1)
            total = total + (value << place)
        return pl.multiple_of(total * size, size)

    for n in range(1 << len(free)):
        span = pl.ds(block_at(n, every), size)
        left = jnp.concatenate([ref[:, span] for ref in refs[:lefts]], axis=0)
        total = matmul(left.T, right)
        for ref, kept in zip(refs[lefts + rights :], waits):
            total = total + ref[pl.ds(block_at(n, kept), size), :].astype(jnp.float32)
        out_ref[n * size : (n + 1) * size, :] = total.astype(out_ref.dtype)


def weight_blocks(here, lefts, rights, fixed, free, waiting, size, dtype, earlier=()):
    blocks = 1 << len(free)
    columns = rights[0].shape[1]
    tokens = sum(item.shape[0] for item in rights)
    out = shape_of((blocks * size, columns), dtype)
    arrays = [item for item, _ in waiting]
    return pl.pallas_call(
        functools.partial(
            weight_kernel,
            lefts=len(lefts),
            rights=len(rights),
            known=dict(fixed),
            free=list(free),
            waits=[kept for _, kept in waiting],
            size=size,
        ),
        out_shape=out,
        in_specs=[whole_smem]
        + [whole_vmem] * (len(lefts) + len(rights) + len(arrays))
        + [pl.BlockSpec(memory_space=pl.ANY)] * len(earlier),
        out_specs=whole_vmem,
        compiler_params=parameters(20 * 2**20),
        cost_estimate=cost(
            2 * tokens * blocks * size * columns, 0, out, *lefts, *rights, *arrays
        ),
        name="weight_blocks",
    )(here, *lefts, *rights, *arrays, *earlier)


class WeightSum:
    def __init__(self, here, lefts, rights, order, fixed=()):
        self.here = here
        self.lefts = lefts
        self.rights = rights
        self.bits = list(order)
        self.known = [(bit, 0) for bit in fixed]
        self.waiting = []
        self.size = lefts[0].shape[1] // lax.axis_size("dp")
        self.plain = self.size % HEAD != 0
        self.fixed = fixed
        self.last = lefts[0]

    def send(self, earlier):
        bit = self.bits.pop(0)
        away = weight_blocks(
            self.here,
            self.lefts,
            self.rights,
            [*self.known, (bit, 1)],
            self.bits,
            self.waiting,
            self.size,
            low_type,
            earlier,
        )
        self.known.append((bit, 0))
        return away, bit

    def receive(self, away, bit):
        self.last = away
        self.waiting.append((flip(away, "dp", 1 << bit), list(self.bits)))

    def step(self, *earlier):
        if not self.plain:
            self.receive(*self.send(earlier))

    def finish(self, *earlier):
        if not self.plain:
            return weight_blocks(
                self.here,
                self.lefts,
                self.rights,
                self.known,
                [],
                self.waiting,
                self.size,
                jnp.float32,
                earlier,
            )
        dp = lax.axis_index("dp")
        left = jnp.concatenate(self.lefts)
        for bit in self.fixed:
            left = left.reshape(left.shape[0], -1, 2, self.size << bit)
            left = pick(left, 2, bit_of(dp, bit)).reshape(left.shape[0], -1)
        return reduce_weight_plain(
            [(left, jnp.concatenate(self.rights))], self.bits, dp
        )


def gelu_parts(gate):
    root = 0.7978845608028654
    square = gate * gate
    curve = jnp.tanh(root * gate * (1.0 + 0.044715 * square))
    half = 0.5 * (1.0 + curve)
    slope = half + 0.5 * gate * (1.0 - curve * curve) * root * (1.0 + 3 * 0.044715 * square)
    return gate * half, slope


def norm_back(grad, scaled, factor, gain):
    grad_scaled = grad * gain
    inner = jnp.mean(grad_scaled * scaled, axis=-1, keepdims=True)
    return factor * (grad_scaled - scaled * inner)


def to_float(value):
    return value.astype(jnp.float32)


def per_device(
    block_input,
    cotangent,
    sequence_blocks,
    gain_attention,
    query_weight,
    keyval_weight,
    output_weight,
    gain_feedforward,
    gate_weight,
    up_weight,
    down_weight,
):
    count = lax.axis_size("dp")
    bits = count.bit_length() - 1
    dp = lax.axis_index("dp")
    rank = lax.axis_index("tensor")
    rows = block_input.shape[0]
    width = block_input.shape[1]
    top = bits - 1
    here = jnp.stack([dp, rank >> 1, rank & 1, rank]).astype(jnp.int32)
    lengths = sequence_blocks
    lane = jnp.arange(HEAD, dtype=jnp.float32) % (HEAD // 2)
    frequency = (10000.0 ** (-lane * 2.0 / HEAD))[None, :]

    def core(value):
        return flip(value, "tensor", 1)

    def over(value):
        return flip(value, "tensor", 2)

    own_normed, own_keyval = opening(
        here, lengths, block_input, gain_attention, keyval_weight, frequency, count
    )
    keyval_over = flip(own_keyval, "tensor", 2)
    near = stack([own_keyval, keyval_over])
    cosine, sine = tables(here, lengths, frequency, own_keyval, count)
    normed = [own_normed, core(own_normed), over(after(own_normed, near))]
    normed.append(core(normed[2]))
    spread = stack([near] + [shift(near, k) for k in range(1, SPANS)])
    across = flip(spread, "tensor", 1)
    keyvals = [spread, across]
    query_0 = project(normed[:2], query_weight, cosine, sine, 0)
    query_1 = project(normed[2:], query_weight, cosine, sine, 1)

    late_cotangent = after(cotangent, spread)
    cotangents = gather_tensor(late_cotangent)
    cotangent_far = flip(late_cotangent, "dp", 1 << top)

    even_1, odd_1, attended_1, logs_1 = attend(
        here, lengths, query_1, output_weight, keyvals, 1, count
    )
    even_0, odd_0, attended_0, logs_0 = attend(
        here, lengths, after(query_0, even_1), output_weight, keyvals, 0, count
    )

    def scatter(even_front, odd_front, even_back, odd_back):
        far = to_float(even_back) + to_float(flip(odd_back, "tensor", 1))
        near = to_float(even_front) + to_float(flip(odd_front, "tensor", 1))
        return near + to_float(flip(far.astype(low_type), "tensor", 2))

    own_input = to_float(block_input)
    own_hidden = own_input + scatter(even_0, odd_0, even_1, odd_1)
    factor_two = lax.rsqrt(jnp.mean(own_hidden * own_hidden, axis=-1, keepdims=True) + epsilon)
    scaled_two = own_hidden * factor_two
    own_normed_two = (scaled_two * gain_feedforward).astype(low_type)
    grad_hidden = grad_product(
        [after(cotangents[0], even_0), *cotangents[1:]], down_weight
    )
    normed_two = gather_tensor(own_normed_two)
    far_two = flip(own_normed_two, "dp", 1 << top)

    hidden_0, grad_gate_0, grad_up_0, back_even_0, back_odd_0 = feed(
        normed_two[:2], grad_hidden, 0, gate_weight, up_weight, True
    )
    hidden_1, grad_gate_1, grad_up_1, back_even_1, back_odd_1 = feed(
        [after(normed_two[2], back_even_0), normed_two[3]], grad_hidden, 1, gate_weight, up_weight, True
    )
    normed_two_far = gather_tensor(after(far_two, normed_two[2]))
    cotangents_far = gather_tensor(after(cotangent_far, own_normed_two))
    far_part = (to_float(back_even_1) + to_float(core(back_odd_1))).astype(low_type)
    near_part = to_float(back_even_0) + to_float(core(back_odd_0))
    own_grad_two = near_part + to_float(over(far_part))
    own_grad_hidden = to_float(cotangent) + norm_back(
        own_grad_two, scaled_two, factor_two, gain_feedforward
    )
    own_grad_low = own_grad_hidden.astype(low_type)
    grad_attention = gather_tensor(own_grad_low)
    grad_hidden_far = grad_product(
        [after(cotangents_far[0], far_part), *cotangents_far[1:]], down_weight
    )
    hidden_far, grad_gate_far, grad_up_far = feed(
        [after(normed_two_far[0], own_grad_low), *normed_two_far[1:]],
        grad_hidden_far,
        0,
        gate_weight,
        up_weight,
        False,
    )

    both_normed_two = [*normed_two, *normed_two_far]
    low_order = list(range(top))
    down_sum = WeightSum(
        here,
        [*cotangents, *cotangents_far],
        [hidden_0, hidden_1, hidden_far],
        low_order[::-1],
        (top,),
    )
    gate_sum = WeightSum(
        here, both_normed_two, [grad_gate_0, grad_gate_1, grad_gate_far], low_order, (top,)
    )
    up_sum = WeightSum(
        here, both_normed_two, [grad_up_0, grad_up_1, grad_up_far], low_order, (top,)
    )
    sums = (gate_sum, down_sum, up_sum)
    for item in sums:
        item.step()

    back_even_0, back_odd_0, grad_query_0, window_keys, window_values = retreat(
        here,
        lengths,
        grad_attention[:2],
        query_weight,
        output_weight,
        keyvals,
        cosine,
        sine,
        query_0,
        attended_0,
        logs_0,
        None,
        0,
        count,
    )
    back_even_1, back_odd_1, grad_query_1, keep_0, keep_2, away = retreat(
        here,
        lengths,
        grad_attention[2:],
        query_weight,
        output_weight,
        keyvals,
        cosine,
        sine,
        query_1,
        attended_1,
        logs_1,
        [window_keys, window_values],
        1,
        count,
    )
    arrived = flip(away, "tensor", 1)
    far_returns = (keep_2 + to_float(arrived[1])).astype(low_type)
    own_returns = keep_0 + to_float(arrived[0]) + to_float(flip(far_returns, "tensor", 2))
    back = [shift(own_returns[k].astype(low_type), -k) for k in range(1, SPANS)]
    own_grad_keyval = return_keyval(here, lengths, back, frequency, own_returns[:1], count)

    query_sum = WeightSum(here, normed, [grad_query_0, grad_query_1], [*low_order, top])
    output_sum = WeightSum(here, grad_attention, [attended_0, attended_1], [*low_order[::-1], top])
    gate_sum.step(far_returns)
    down_sum.step(gate_sum.last)
    output_sum.step(down_sum.last)
    up_sum.step(own_returns, output_sum.last)
    own_grad_one = scatter(back_even_0, back_odd_0, back_even_1, back_odd_1) + times_transposed(
        own_grad_keyval, keyval_weight
    )
    factor_one = lax.rsqrt(jnp.mean(own_input * own_input, axis=-1, keepdims=True) + epsilon)
    grad_rows = own_grad_hidden + norm_back(
        own_grad_one, own_input * factor_one, factor_one, gain_attention
    )

    quarter = 2 * HEAD // 4
    grad_keyval = jnp.concatenate(gather_tensor(own_grad_keyval))
    part = lax.dynamic_slice_in_dim(grad_keyval, rank * quarter, quarter, 1)
    keyval_sum = WeightSum(here, normed, [part], [*low_order, top])
    keyval_sum.step()
    query_sum.step(keyval_sum.last)
    for _ in range(bits - 1):
        keyval_sum.step()
    pieces = jnp.stack(gather_tensor(keyval_sum.finish().T))
    pieces = [pick(pieces, 0, rank ^ g).reshape(quarter, -1) for g in range(4)]
    grad_keyval_weight = jnp.concatenate(pieces).T

    for item in (output_sum, query_sum, gate_sum, down_sum, up_sum):
        for _ in range(len(item.bits)):
            item.step()
    grad_down = down_sum.finish()
    grad_gate_weight = gate_sum.finish()
    grad_up_weight = up_sum.finish()
    grad_query_weight = query_sum.finish()
    grad_output_weight = output_sum.finish()

    down_front = times_transposed(after(hidden_0, own_returns), down_weight).astype(low_type)
    down_back = times_transposed(after(hidden_1, own_returns), down_weight).astype(low_type)
    block_output = (
        own_hidden
        + scatter(down_front[:rows], down_front[rows:], down_back[:rows], down_back[rows:])
    ).astype(low_type)

    size = width // count

    def own_block(value):
        return lax.dynamic_slice_in_dim(value, dp * size, size, 0)

    def sum_tensor(value):
        value = value + flip(value, "tensor", 1)
        return value + flip(value, "tensor", 2)

    gain_two = sum_tensor(
        jnp.sum(to_float(own_block(gate_weight)) * grad_gate_weight, axis=1)
        + jnp.sum(to_float(own_block(up_weight)) * grad_up_weight, axis=1)
    ) / own_block(gain_feedforward)
    gain_one = (
        sum_tensor(jnp.sum(to_float(own_block(query_weight)) * grad_query_weight, axis=1))
        + jnp.sum(to_float(own_block(keyval_weight)) * grad_keyval_weight, axis=1)
    ) / own_block(gain_attention)
    return (
        block_output,
        grad_rows,
        gain_one,
        grad_query_weight,
        grad_keyval_weight,
        grad_output_weight,
        gain_two,
        grad_gate_weight,
        grad_up_weight,
        grad_down,
    )


def solution(mesh):
    placed = (
        P(("dp", "tensor"), None),
        P(("dp", "tensor"), None),
        P(),
        P(),
        P(None, "tensor"),
        P(),
        P(None, "tensor"),
        P(),
        P(None, "tensor"),
        P(None, "tensor"),
        P(None, "tensor"),
    )
    return jax.shard_map(
        per_device,
        mesh=mesh,
        in_specs=placed,
        out_specs=(
            P(("dp", "tensor"), None),
            P(("dp", "tensor"), None),
            P("dp"),
            P("dp", "tensor"),
            P("dp", None),
            P("dp", "tensor"),
            P("dp"),
            P("dp", "tensor"),
            P("dp", "tensor"),
            P("dp", "tensor"),
        ),
        check_vma=False,
    )
```

```python
import functools

import jax
import jax.numpy as jnp
from jax import lax
from jax.experimental import pallas as pl
from jax.experimental.pallas import tpu as pltpu
from jax.sharding import PartitionSpec as P

HEAD = 128
WINDOW = 1024
BLOCK = 256
SPANS = WINDOW // BLOCK + 1

epsilon = 1e-06
negative = -1e30
low_type = jnp.bfloat16


def matmul(left, right):
    return jnp.dot(left, right, preferred_element_type=jnp.float32)


def times_transposed(left, right):
    return lax.dot_general(
        left, right, (((1,), (1,)), ((), ())), preferred_element_type=jnp.float32
    )


def outer_sum(left, right):
    return lax.dot_general(
        left, right, (((0,), (0,)), ((), ())), preferred_element_type=jnp.float32
    )


def flip(value, axis, bit):
    count = lax.axis_size(axis)
    return lax.ppermute(value, axis, [(i, i ^ bit) for i in range(count)])


def shift(value, step):
    count = lax.axis_size("dp")
    return lax.ppermute(value, "dp", [(i, (i + step) % count) for i in range(count)])


def gather_tensor(value):
    over = flip(value, "tensor", 2)
    return [value, flip(value, "tensor", 1), over, flip(over, "tensor", 1)]


def bit_of(index, bit):
    return (index >> bit) & 1


def pick(value, axis, index):
    return lax.dynamic_index_in_dim(value, index, axis, keepdims=False)


def reduce_weight_plain(pairs, order, dp):
    count = lax.axis_size("dp")
    bits = sorted(order, reverse=True)
    lefts = []
    for left, _ in pairs:
        lefts.append(left.reshape(left.shape[0], *([2] * len(bits)), -1))
    rights = [right for _, right in pairs]
    size = lefts[0].shape[-1]
    width = rights[0].shape[1]
    pending = []

    def product(chosen, waiting):
        total = None
        for left, right in zip(chosen, rights):
            part = outer_sum(left.reshape(left.shape[0], -1), right)
            total = part if total is None else total + part
        for item in waiting:
            total = total + item.reshape(total.shape).astype(jnp.float32)
        return total

    for bit in order:
        place = bits.index(bit)
        mine = bit_of(dp, bit)
        away = product(
            [pick(left, place + 1, 1 - mine) for left in lefts],
            [pick(item, place, 1 - mine) for item in pending],
        ).astype(low_type)
        arrived = flip(away, "dp", 1 << bit)
        bits.remove(bit)
        lefts = [pick(left, place + 1, mine) for left in lefts]
        pending = [pick(item, place, mine) for item in pending]
        pending.append(arrived.reshape(*([2] * len(bits)), size, width))
    return product(lefts, pending)


vmem_limit = 16 * 2**20
log2e = 1.4426950408889634
whole_vmem = pl.BlockSpec(memory_space=pltpu.VMEM)
whole_smem = pl.BlockSpec(memory_space=pltpu.SMEM)


def after(value, *others):
    return lax.optimization_barrier((value, *others))[0]


def cost(flops, transcendentals, *arrays):
    total = 0
    for item in arrays:
        total += item.size * item.dtype.itemsize
    return pl.CostEstimate(
        flops=int(flops), transcendentals=int(transcendentals), bytes_accessed=int(total)
    )


def parameters(limit=vmem_limit):
    return pltpu.CompilerParams(vmem_limit_bytes=limit)


def shape_of(shape, dtype):
    return jax.ShapeDtypeStruct(shape, dtype)


def turn(values, cosine, sine):
    return values * cosine + pltpu.roll(values, HEAD // 2, 1) * sine


def slot_facts(here, lengths, u, count):
    dp = here[0]
    slot = here[1] ^ u
    number = dp + slot * count
    start = jnp.int32(0)
    end = jnp.int32(0)
    for n in range(lengths.shape[0]):
        end = end + lengths[n]
        start = jnp.where(end <= number, end, start)
    pairs = [
        (slot if k == 0 else jnp.where(dp >= k, slot, 0)) ^ here[1] for k in range(SPANS)
    ]
    return number - start, pairs


def angle_tables(block, side, frequency, rows):
    place = lax.broadcasted_iota(jnp.int32, (rows, HEAD), 0) ^ (side * (BLOCK // 2))
    lane = lax.broadcasted_iota(jnp.int32, (rows, HEAD), 1)
    angle = (block * BLOCK + place).astype(jnp.float32) * frequency
    sine = jnp.sin(angle)
    return jnp.cos(angle), jnp.where(lane < HEAD // 2, -sine, sine)


def opening_kernel(
    here, lengths, x_ref, gain_ref, weight_ref, frequency_ref, normed_ref, keyval_ref, *, count
):
    x = x_ref[...].astype(jnp.float32)
    factor = lax.rsqrt(jnp.mean(x * x, axis=-1, keepdims=True) + epsilon)
    normed = (x * factor * gain_ref[...]).astype(low_type)
    normed_ref[...] = normed
    keyval = matmul(normed, weight_ref[...])
    block, _ = slot_facts(here, lengths, 0, count)
    cosine, sine = angle_tables(block, here[2], frequency_ref[...], x.shape[0])
    keyval_ref[:, :HEAD] = turn(keyval[:, :HEAD], cosine, sine).astype(low_type)
    keyval_ref[:, HEAD:] = keyval[:, HEAD:].astype(low_type)


def opening(here, lengths, x, gain, weight, frequency, count):
    outs = (
        shape_of(x.shape, low_type),
        shape_of((x.shape[0], weight.shape[1]), low_type),
    )
    return pl.pallas_call(
        functools.partial(opening_kernel, count=count),
        out_shape=outs,
        in_specs=[whole_smem] * 2 + [whole_vmem] * 4,
        out_specs=(whole_vmem, whole_vmem),
        compiler_params=parameters(),
        cost_estimate=cost(2 * x.size * weight.shape[1], x.shape[0], x, weight, *outs),
        name="opening",
    )(here, lengths, x, gain.reshape(1, -1), weight, frequency)


def tables_kernel(here, lengths, frequency_ref, normed_ref, cosine_ref, sine_ref, *, count):
    del normed_ref
    for u in range(2):
        block, _ = slot_facts(here, lengths, u, count)
        cosine, sine = angle_tables(block, here[2], frequency_ref[...], BLOCK)
        cosine_ref[u] = cosine
        sine_ref[u] = sine


def tables(here, lengths, frequency, earlier, count):
    out = shape_of((2, BLOCK, HEAD), jnp.float32)
    return pl.pallas_call(
        functools.partial(tables_kernel, count=count),
        out_shape=(out, out),
        in_specs=[whole_smem] * 2 + [whole_vmem, pl.BlockSpec(memory_space=pl.ANY)],
        out_specs=(whole_vmem, whole_vmem),
        compiler_params=parameters(),
        cost_estimate=cost(100 * out.size, 0, out, out),
        name="tables",
    )(here, lengths, frequency, earlier)


def project_kernel(normed_a, normed_b, weight_ref, cosine_ref, sine_ref, query_ref, *, u):
    normed = jnp.concatenate([normed_a[...], normed_b[...]], axis=0)
    raw = matmul(normed, weight_ref[...])
    for head in range(raw.shape[1] // HEAD):
        at = slice(head * HEAD, (head + 1) * HEAD)
        query_ref[:, at] = turn(raw[:, at], cosine_ref[u], sine_ref[u]).astype(low_type)


def project(normed, weight, cosine, sine, u):
    rows, width = normed[0].shape
    columns = weight.shape[1]
    out = shape_of((2 * rows, columns), low_type)
    return pl.pallas_call(
        functools.partial(project_kernel, u=u),
        out_shape=out,
        in_specs=[whole_vmem] * 5,
        out_specs=whole_vmem,
        compiler_params=parameters(),
        cost_estimate=cost(4 * rows * width * columns, 0, *normed, weight, out),
        name="project",
    )(*normed, weight, cosine, sine)


def stack_kernel(*refs):
    *parts, out_ref = refs
    for k, part in enumerate(parts):
        out_ref[k] = part[...]


def stack(parts):
    out = shape_of((len(parts), *parts[0].shape), parts[0].dtype)
    return pl.pallas_call(
        stack_kernel,
        out_shape=out,
        in_specs=[whole_vmem] * len(parts),
        out_specs=whole_vmem,
        compiler_params=parameters(),
        cost_estimate=cost(0, 0, out, out),
        name="stack",
    )(*parts)


def fill_window(pairs, keyvals, keys, values):
    half = BLOCK // 2
    for k in range(SPANS):
        for side in range(2):
            block = keyvals[side][k, pairs[k]]
            at = k * BLOCK + side * half
            keys[at : at + half, :] = block[:, :HEAD]
            values[at : at + half, :] = block[:, HEAD:]


def window_masks(block, side):
    swap = side * (BLOCK // 2)
    keys = lax.broadcasted_iota(jnp.int32, (BLOCK, BLOCK), 0) ^ swap
    rows = lax.broadcasted_iota(jnp.int32, (BLOCK, BLOCK), 1) ^ swap
    beyond = jnp.where(block >= SPANS - 1, 0, BLOCK)
    return keys <= rows, keys > rows + beyond


def masked(scores, k, masks, block):
    if k == 0:
        return jnp.where(masks[0], scores, negative)
    if k == SPANS - 1:
        return jnp.where(masks[1], scores, negative)
    return scores + jnp.where(block >= k, 0.0, negative)


def attend_kernel(
    here,
    lengths,
    query_ref,
    output_weight,
    keyval_0,
    keyval_1,
    even_ref,
    odd_ref,
    attended_ref,
    log_ref,
    keys,
    values,
    *,
    heads,
    u,
    count,
):
    block, pairs = slot_facts(here, lengths, u, count)
    fill_window(pairs, (keyval_0, keyval_1), keys, values)
    masks = window_masks(block, here[2])
    values_turned = values[...].T
    factor = HEAD ** (-0.5) * log2e
    for head in range(heads):
        at = slice(head * HEAD, (head + 1) * HEAD)
        query = query_ref[:, at]
        scores = []
        for k in range(SPANS):
            part = times_transposed(keys[k * BLOCK : (k + 1) * BLOCK, :], query) * factor
            scores.append(masked(part, k, masks, block))
        peak = jnp.max(scores[0], axis=0, keepdims=True)
        for part in scores[1:]:
            peak = jnp.maximum(peak, jnp.max(part, axis=0, keepdims=True))
        exponents = [jnp.exp2(part - peak) for part in scores]
        total = jnp.sum(exponents[0], axis=0, keepdims=True)
        for part in exponents[1:]:
            total = total + jnp.sum(part, axis=0, keepdims=True)
        inverse = 1.0 / total
        log_ref[head : head + 1, :] = peak + jnp.log(total) * log2e
        soft = jnp.concatenate([(part * inverse).astype(low_type) for part in exponents], axis=0)
        attended_ref[:, at] = matmul(values_turned, soft).T.astype(low_type)
    part = times_transposed(attended_ref[...], output_weight[...]).astype(low_type)
    even_ref[...] = part[: BLOCK // 2]
    odd_ref[...] = part[BLOCK // 2 :]


def attend(here, lengths, query, output_weight, keyvals, u, count):
    width, columns = output_weight.shape
    heads = columns // HEAD
    outs = (
        shape_of((BLOCK // 2, width), low_type),
        shape_of((BLOCK // 2, width), low_type),
        shape_of((BLOCK, columns), low_type),
        shape_of((8, BLOCK), jnp.float32),
    )
    flops = 2 * BLOCK * width * columns + 4 * BLOCK * SPANS * BLOCK * columns
    return pl.pallas_call(
        functools.partial(attend_kernel, heads=heads, u=u, count=count),
        out_shape=outs,
        in_specs=[whole_smem] * 2 + [whole_vmem] * 4,
        out_specs=(whole_vmem,) * 4,
        scratch_shapes=[pltpu.VMEM((SPANS * BLOCK, HEAD), low_type)] * 2,
        compiler_params=parameters(),
        cost_estimate=cost(
            flops, heads * SPANS * BLOCK * BLOCK, output_weight, *keyvals, *outs
        ),
        name="attend",
    )(here, lengths, query, output_weight, *keyvals)


def retreat_kernel(
    here,
    lengths,
    grad_a,
    grad_b,
    query_weight,
    output_weight,
    keyval_0,
    keyval_1,
    cosine_ref,
    sine_ref,
    query_ref,
    attended_ref,
    log_ref,
    *rest,
    heads,
    closing,
    u,
    count,
):
    block, pairs = slot_facts(here, lengths, u, count)
    if closing:
        other_keys, other_values = rest[:2]
        rest = rest[2:]
        even_ref, odd_ref, grad_query_ref, keep_0, keep_2, away = rest[:6]
        rest = rest[6:]
    else:
        even_ref, odd_ref, grad_query_ref, grad_keys, grad_values = rest[:5]
        rest = rest[5:]
    keys, values = rest[:2]
    if closing:
        grad_keys, grad_values = rest[2:4]
    fill_window(pairs, (keyval_0, keyval_1), keys, values)
    masks = window_masks(block, here[2])
    grad = jnp.concatenate([grad_a[...], grad_b[...]], axis=0)
    grad_attended = matmul(grad, output_weight[...]).astype(low_type)
    keys_turned = keys[...].T
    scale = HEAD ** (-0.5)
    factor = scale * log2e
    for head in range(heads):
        at = slice(head * HEAD, (head + 1) * HEAD)
        query = query_ref[:, at]
        grad_head = grad_attended[:, at]
        inner = jnp.sum(
            (grad_head.astype(jnp.float32) * attended_ref[:, at].astype(jnp.float32)).T,
            axis=0,
            keepdims=True,
        )
        log_row = log_ref[head : head + 1, :]
        grad_query = None
        for k in range(SPANS):
            span = slice(k * BLOCK, (k + 1) * BLOCK)
            part = times_transposed(keys[span, :], query) * factor
            soft = jnp.exp2(masked(part, k, masks, block) - log_row)
            grad_soft = times_transposed(values[span, :], grad_head)
            grad_scores = (soft * (grad_soft - inner)).astype(low_type)
            grad_key = matmul(grad_scores, query)
            grad_value = matmul(soft.astype(low_type), grad_head)
            if head == 0:
                grad_keys[span, :] = grad_key
                grad_values[span, :] = grad_value
            else:
                grad_keys[span, :] += grad_key
                grad_values[span, :] += grad_value
            step = matmul(keys_turned[:, span], grad_scores)
            grad_query = step if grad_query is None else grad_query + step
        grad_query_ref[:, at] = turn(
            grad_query.T * scale, cosine_ref[u], -sine_ref[u]
        ).astype(low_type)
    part = times_transposed(grad_query_ref[...], query_weight[...]).astype(low_type)
    even_ref[...] = part[: BLOCK // 2]
    odd_ref[...] = part[BLOCK // 2 :]
    if closing:
        _, other_pairs = slot_facts(here, lengths, 1 - u, count)
        half = BLOCK // 2
        for k in range(SPANS):
            for pair in range(2):
                mine = jnp.where(pairs[k] == pair, 1.0, 0.0)
                other = jnp.where(other_pairs[k] == pair, 1.0, 0.0)
                for side in range(2):
                    span = slice(k * BLOCK + side * half, k * BLOCK + (side + 1) * half)
                    key = (grad_keys[span, :] * mine + other_keys[span, :] * other) * scale
                    value = grad_values[span, :] * mine + other_values[span, :] * other
                    if side == 1:
                        away[pair, k, :, :HEAD] = key.astype(low_type)
                        away[pair, k, :, HEAD:] = value.astype(low_type)
                    else:
                        keep = keep_2 if pair else keep_0
                        keep[k, :, :HEAD] = key
                        keep[k, :, HEAD:] = value


def retreat(
    here,
    lengths,
    grads,
    query_weight,
    output_weight,
    keyvals,
    cosine,
    sine,
    query,
    attended,
    logs,
    other,
    u,
    count,
):
    rows, width = grads[0].shape
    columns = query_weight.shape[1]
    heads = columns // HEAD
    closing = other is not None
    outs = [
        shape_of((rows, width), low_type),
        shape_of((rows, width), low_type),
        shape_of((BLOCK, columns), low_type),
    ]
    window = (SPANS * BLOCK, HEAD)
    scratch = [pltpu.VMEM(window, low_type)] * 2
    operands = [
        here, lengths, *grads, query_weight, output_weight, *keyvals, cosine, sine, query,
        attended, logs,
    ]
    in_specs = [whole_smem] * 2 + [whole_vmem] * 11
    if closing:
        outs += [
            shape_of((SPANS, rows, 2 * HEAD), jnp.float32),
            shape_of((SPANS, rows, 2 * HEAD), jnp.float32),
            shape_of((2, SPANS, rows, 2 * HEAD), low_type),
        ]
        scratch += [pltpu.VMEM(window, jnp.float32)] * 2
        operands += other
        in_specs += [whole_vmem] * 2
    else:
        outs += [shape_of(window, jnp.float32)] * 2
    flops = 4 * BLOCK * width * columns + 10 * BLOCK * SPANS * BLOCK * columns
    return pl.pallas_call(
        functools.partial(retreat_kernel, heads=heads, closing=closing, u=u, count=count),
        out_shape=tuple(outs),
        in_specs=in_specs,
        out_specs=(whole_vmem,) * len(outs),
        scratch_shapes=scratch,
        compiler_params=parameters(20 * 2**20),
        cost_estimate=cost(
            flops, heads * SPANS * BLOCK * BLOCK, query_weight, output_weight, *keyvals, *outs
        ),
        name="retreat",
    )(*operands)


def return_kernel(here, lengths, *refs, count):
    *parts, frequency_ref, own_ref, out_ref = refs
    total = own_ref[0]
    for part in parts:
        total = total + part[...].astype(jnp.float32)
    block, _ = slot_facts(here, lengths, 0, count)
    cosine, sine = angle_tables(block, here[2], frequency_ref[...], total.shape[0])
    out_ref[:, :HEAD] = turn(total[:, :HEAD], cosine, -sine).astype(low_type)
    out_ref[:, HEAD:] = total[:, HEAD:].astype(low_type)


def return_keyval(here, lengths, parts, frequency, own, count):
    out = shape_of(parts[0].shape, low_type)
    return pl.pallas_call(
        functools.partial(return_kernel, count=count),
        out_shape=out,
        in_specs=[whole_smem] * 2 + [whole_vmem] * (len(parts) + 2),
        out_specs=whole_vmem,
        compiler_params=parameters(),
        cost_estimate=cost(0, out.size, out, *parts, own),
        name="return_keyval",
    )(here, lengths, *parts, frequency, own)


def column_tiles(columns, most=512):
    size = most
    while columns % size:
        size //= 2
    return [slice(at, at + size) for at in range(0, columns, size)]


def grad_product_kernel(*refs):
    *parts, weight_ref, out_ref = refs
    rows = jnp.concatenate([part[...] for part in parts], axis=0)
    for at in column_tiles(weight_ref.shape[1]):
        out_ref[:, at] = matmul(rows, weight_ref[:, at])


def grad_product(parts, weight):
    rows, width = parts[0].shape
    columns = weight.shape[1]
    out = shape_of((rows * len(parts), columns), jnp.float32)
    return pl.pallas_call(
        grad_product_kernel,
        out_shape=out,
        in_specs=[whole_vmem] * (len(parts) + 1),
        out_specs=whole_vmem,
        compiler_params=parameters(),
        cost_estimate=cost(2 * rows * len(parts) * width * columns, 0, *parts, weight, out),
        name="grad_product",
    )(*parts, weight)


def feed_kernel(*refs, count, grad_at, closing):
    parts = refs[:count]
    grad_ref, gate_ref, up_ref = refs[count : count + 3]
    hidden_ref, grad_gate_ref, grad_up_ref = refs[count + 3 : count + 6]
    rows = jnp.concatenate([part[...] for part in parts], axis=0)
    total_rows = rows.shape[0]
    for at in column_tiles(gate_ref.shape[1]):
        gate = matmul(rows, gate_ref[:, at])
        upper = matmul(rows, up_ref[:, at])
        grad = grad_ref[grad_at * total_rows : (grad_at + 1) * total_rows, at]
        activated, slope = gelu_parts(gate)
        hidden_ref[:, at] = (activated * upper).astype(low_type)
        grad_gate_ref[:, at] = (grad * upper * slope).astype(low_type)
        grad_up_ref[:, at] = (grad * activated).astype(low_type)
    if closing:
        even_ref, odd_ref = refs[count + 6 :]
        size = even_ref.shape[0]
        for at in column_tiles(gate_ref.shape[0]):
            total = times_transposed(grad_gate_ref[...], gate_ref[at, :]) + times_transposed(
                grad_up_ref[...], up_ref[at, :]
            )
            even_ref[:, at] = total[:size].astype(low_type)
            odd_ref[:, at] = total[size:].astype(low_type)


def feed(parts, grad, grad_at, gate_weight, up_weight, closing):
    rows, width = parts[0].shape
    columns = gate_weight.shape[1]
    total_rows = rows * len(parts)
    outs = [shape_of((total_rows, columns), low_type)] * 3
    if closing:
        outs += [shape_of((rows, width), low_type)] * 2
    flops = (8 if closing else 4) * total_rows * width * columns
    return pl.pallas_call(
        functools.partial(feed_kernel, count=len(parts), grad_at=grad_at, closing=closing),
        out_shape=tuple(outs),
        in_specs=[whole_vmem] * (len(parts) + 3),
        out_specs=(whole_vmem,) * len(outs),
        compiler_params=parameters(24 * 2**20),
        cost_estimate=cost(flops, total_rows * columns, gate_weight, up_weight, *outs, *outs[:1]),
        name="feed_back" if closing else "feed",
    )(*parts, grad, gate_weight, up_weight)


def weight_kernel(here, *refs, lefts, rights, known, free, waits, size):
    right = jnp.concatenate([ref[...] for ref in refs[lefts : lefts + rights]], axis=0)
    out_ref = refs[-1]
    every = sorted([*known, *free])

    def block_at(n, kept):
        total = jnp.int32(0)
        for place, bit in enumerate(kept):
            if bit in known:
                value = ((here[0] >> bit) & 1) ^ known[bit]
            else:
                value = jnp.int32((n >> free.index(bit)) & 1)
            total = total + (value << place)
        return pl.multiple_of(total * size, size)

    for n in range(1 << len(free)):
        span = pl.ds(block_at(n, every), size)
        left = jnp.concatenate([ref[:, span] for ref in refs[:lefts]], axis=0)
        total = matmul(left.T, right)
        for ref, kept in zip(refs[lefts + rights :], waits):
            total = total + ref[pl.ds(block_at(n, kept), size), :].astype(jnp.float32)
        out_ref[n * size : (n + 1) * size, :] = total.astype(out_ref.dtype)


def weight_blocks(here, lefts, rights, fixed, free, waiting, size, dtype, earlier=()):
    blocks = 1 << len(free)
    columns = rights[0].shape[1]
    tokens = sum(item.shape[0] for item in rights)
    out = shape_of((blocks * size, columns), dtype)
    arrays = [item for item, _ in waiting]
    return pl.pallas_call(
        functools.partial(
            weight_kernel,
            lefts=len(lefts),
            rights=len(rights),
            known=dict(fixed),
            free=list(free),
            waits=[kept for _, kept in waiting],
            size=size,
        ),
        out_shape=out,
        in_specs=[whole_smem]
        + [whole_vmem] * (len(lefts) + len(rights) + len(arrays))
        + [pl.BlockSpec(memory_space=pl.ANY)] * len(earlier),
        out_specs=whole_vmem,
        compiler_params=parameters(20 * 2**20),
        cost_estimate=cost(
            2 * tokens * blocks * size * columns, 0, out, *lefts, *rights, *arrays
        ),
        name="weight_blocks",
    )(here, *lefts, *rights, *arrays, *earlier)


class WeightSum:
    def __init__(self, here, lefts, rights, order, fixed=()):
        self.here = here
        self.lefts = lefts
        self.rights = rights
        self.bits = list(order)
        self.known = [(bit, 0) for bit in fixed]
        self.waiting = []
        self.size = lefts[0].shape[1] // lax.axis_size("dp")
        self.plain = self.size % HEAD != 0
        self.fixed = fixed
        self.last = lefts[0]

    def send(self, earlier):
        bit = self.bits.pop(0)
        away = weight_blocks(
            self.here,
            self.lefts,
            self.rights,
            [*self.known, (bit, 1)],
            self.bits,
            self.waiting,
            self.size,
            low_type,
            earlier,
        )
        self.known.append((bit, 0))
        return away, bit

    def receive(self, away, bit):
        self.last = away
        self.waiting.append((flip(away, "dp", 1 << bit), list(self.bits)))

    def step(self, *earlier):
        if not self.plain:
            self.receive(*self.send(earlier))

    def finish(self, *earlier):
        if not self.plain:
            return weight_blocks(
                self.here,
                self.lefts,
                self.rights,
                self.known,
                [],
                self.waiting,
                self.size,
                jnp.float32,
                earlier,
            )
        dp = lax.axis_index("dp")
        left = jnp.concatenate(self.lefts)
        for bit in self.fixed:
            left = left.reshape(left.shape[0], -1, 2, self.size << bit)
            left = pick(left, 2, bit_of(dp, bit)).reshape(left.shape[0], -1)
        return reduce_weight_plain(
            [(left, jnp.concatenate(self.rights))], self.bits, dp
        )


def gelu_parts(gate):
    root = 0.7978845608028654
    square = gate * gate
    curve = jnp.tanh(root * gate * (1.0 + 0.044715 * square))
    half = 0.5 * (1.0 + curve)
    slope = half + 0.5 * gate * (1.0 - curve * curve) * root * (1.0 + 3 * 0.044715 * square)
    return gate * half, slope


def norm_back(grad, scaled, factor, gain):
    grad_scaled = grad * gain
    inner = jnp.mean(grad_scaled * scaled, axis=-1, keepdims=True)
    return factor * (grad_scaled - scaled * inner)


def to_float(value):
    return value.astype(jnp.float32)


def per_device(
    block_input,
    cotangent,
    sequence_blocks,
    gain_attention,
    query_weight,
    keyval_weight,
    output_weight,
    gain_feedforward,
    gate_weight,
    up_weight,
    down_weight,
):
    count = lax.axis_size("dp")
    bits = count.bit_length() - 1
    dp = lax.axis_index("dp")
    rank = lax.axis_index("tensor")
    rows = block_input.shape[0]
    width = block_input.shape[1]
    top = bits - 1
    here = jnp.stack([dp, rank >> 1, rank & 1, rank]).astype(jnp.int32)
    lengths = sequence_blocks
    lane = jnp.arange(HEAD, dtype=jnp.float32) % (HEAD // 2)
    frequency = (10000.0 ** (-lane * 2.0 / HEAD))[None, :]

    def core(value):
        return flip(value, "tensor", 1)

    def over(value):
        return flip(value, "tensor", 2)

    own_normed, own_keyval = opening(
        here, lengths, block_input, gain_attention, keyval_weight, frequency, count
    )
    keyval_over = flip(own_keyval, "tensor", 2)
    near = stack([own_keyval, keyval_over])
    cosine, sine = tables(here, lengths, frequency, own_keyval, count)
    normed = [own_normed, core(own_normed), over(after(own_normed, near))]
    normed.append(core(normed[2]))
    spread = stack([near] + [shift(near, k) for k in range(1, SPANS)])
    across = flip(spread, "tensor", 1)
    keyvals = [spread, across]
    query_0 = project(normed[:2], query_weight, cosine, sine, 0)
    query_1 = project(normed[2:], query_weight, cosine, sine, 1)

    late_cotangent = after(cotangent, spread)
    cotangents = gather_tensor(late_cotangent)
    cotangent_far = flip(late_cotangent, "dp", 1 << top)

    even_1, odd_1, attended_1, logs_1 = attend(
        here, lengths, query_1, output_weight, keyvals, 1, count
    )
    even_0, odd_0, attended_0, logs_0 = attend(
        here, lengths, after(query_0, even_1), output_weight, keyvals, 0, count
    )

    def scatter(even_front, odd_front, even_back, odd_back):
        far = to_float(even_back) + to_float(flip(odd_back, "tensor", 1))
        near = to_float(even_front) + to_float(flip(odd_front, "tensor", 1))
        return near + to_float(flip(far.astype(low_type), "tensor", 2))

    own_input = to_float(block_input)
    own_hidden = own_input + scatter(even_0, odd_0, even_1, odd_1)
    factor_two = lax.rsqrt(jnp.mean(own_hidden * own_hidden, axis=-1, keepdims=True) + epsilon)
    scaled_two = own_hidden * factor_two
    own_normed_two = (scaled_two * gain_feedforward).astype(low_type)
    grad_hidden = grad_product(
        [after(cotangents[0], even_0), *cotangents[1:]], down_weight
    )
    normed_two = gather_tensor(own_normed_two)
    far_two = flip(own_normed_two, "dp", 1 << top)

    hidden_0, grad_gate_0, grad_up_0, back_even_0, back_odd_0 = feed(
        normed_two[:2], grad_hidden, 0, gate_weight, up_weight, True
    )
    hidden_1, grad_gate_1, grad_up_1, back_even_1, back_odd_1 = feed(
        [after(normed_two[2], back_even_0), normed_two[3]], grad_hidden, 1, gate_weight, up_weight, True
    )
    normed_two_far = gather_tensor(after(far_two, normed_two[2]))
    cotangents_far = gather_tensor(after(cotangent_far, own_normed_two))
    far_part = (to_float(back_even_1) + to_float(core(back_odd_1))).astype(low_type)
    near_part = to_float(back_even_0) + to_float(core(back_odd_0))
    own_grad_two = near_part + to_float(over(far_part))
    own_grad_hidden = to_float(cotangent) + norm_back(
        own_grad_two, scaled_two, factor_two, gain_feedforward
    )
    own_grad_low = own_grad_hidden.astype(low_type)
    grad_attention = gather_tensor(own_grad_low)
    grad_hidden_far = grad_product(
        [after(cotangents_far[0], far_part), *cotangents_far[1:]], down_weight
    )
    hidden_far, grad_gate_far, grad_up_far = feed(
        [after(normed_two_far[0], own_grad_low), *normed_two_far[1:]],
        grad_hidden_far,
        0,
        gate_weight,
        up_weight,
        False,
    )

    both_normed_two = [*normed_two, *normed_two_far]
    low_order = list(range(top))
    down_sum = WeightSum(
        here,
        [*cotangents, *cotangents_far],
        [hidden_0, hidden_1, hidden_far],
        low_order[::-1],
        (top,),
    )
    gate_sum = WeightSum(
        here, both_normed_two, [grad_gate_0, grad_gate_1, grad_gate_far], low_order, (top,)
    )
    up_sum = WeightSum(
        here, both_normed_two, [grad_up_0, grad_up_1, grad_up_far], low_order, (top,)
    )
    sums = (gate_sum, down_sum, up_sum)
    for item in sums:
        item.step()

    back_even_0, back_odd_0, grad_query_0, window_keys, window_values = retreat(
        here,
        lengths,
        grad_attention[:2],
        query_weight,
        output_weight,
        keyvals,
        cosine,
        sine,
        query_0,
        attended_0,
        logs_0,
        None,
        0,
        count,
    )
    back_even_1, back_odd_1, grad_query_1, keep_0, keep_2, away = retreat(
        here,
        lengths,
        grad_attention[2:],
        query_weight,
        output_weight,
        keyvals,
        cosine,
        sine,
        query_1,
        attended_1,
        logs_1,
        [window_keys, window_values],
        1,
        count,
    )
    arrived = flip(away, "tensor", 1)
    far_returns = (keep_2 + to_float(arrived[1])).astype(low_type)
    own_returns = keep_0 + to_float(arrived[0]) + to_float(flip(far_returns, "tensor", 2))
    back = [shift(own_returns[k].astype(low_type), -k) for k in range(1, SPANS)]
    own_grad_keyval = return_keyval(here, lengths, back, frequency, own_returns[:1], count)

    query_sum = WeightSum(here, normed, [grad_query_0, grad_query_1], [*low_order, top])
    output_sum = WeightSum(here, grad_attention, [attended_0, attended_1], [*low_order[::-1], top])
    gate_sum.step(far_returns)
    down_sum.step(gate_sum.last)
    output_sum.step(down_sum.last)
    up_sum.step(own_returns)
    own_grad_one = scatter(back_even_0, back_odd_0, back_even_1, back_odd_1) + times_transposed(
        own_grad_keyval, keyval_weight
    )
    factor_one = lax.rsqrt(jnp.mean(own_input * own_input, axis=-1, keepdims=True) + epsilon)
    grad_rows = own_grad_hidden + norm_back(
        own_grad_one, own_input * factor_one, factor_one, gain_attention
    )

    quarter = 2 * HEAD // 4
    grad_keyval = jnp.concatenate(gather_tensor(own_grad_keyval))
    part = lax.dynamic_slice_in_dim(grad_keyval, rank * quarter, quarter, 1)
    keyval_sum = WeightSum(here, normed, [part], [*low_order, top])
    keyval_sum.step()
    query_sum.step(keyval_sum.last)
    keyval_sum.step()
    output_sum.step(keyval_sum.last)
    for _ in range(bits - 2):
        keyval_sum.step(output_sum.last)
    pieces = jnp.stack(gather_tensor(keyval_sum.finish().T))
    pieces = [pick(pieces, 0, rank ^ g).reshape(quarter, -1) for g in range(4)]
    grad_keyval_weight = jnp.concatenate(pieces).T

    for item in (output_sum, query_sum, gate_sum, down_sum, up_sum):
        for _ in range(len(item.bits)):
            item.step()
    grad_down = down_sum.finish()
    grad_gate_weight = gate_sum.finish()
    grad_up_weight = up_sum.finish()
    grad_query_weight = query_sum.finish()
    grad_output_weight = output_sum.finish()

    down_front = times_transposed(after(hidden_0, own_returns), down_weight).astype(low_type)
    down_back = times_transposed(after(hidden_1, own_returns), down_weight).astype(low_type)
    block_output = (
        own_hidden
        + scatter(down_front[:rows], down_front[rows:], down_back[:rows], down_back[rows:])
    ).astype(low_type)

    size = width // count

    def own_block(value):
        return lax.dynamic_slice_in_dim(value, dp * size, size, 0)

    def sum_tensor(value):
        value = value + flip(value, "tensor", 1)
        return value + flip(value, "tensor", 2)

    gain_two = sum_tensor(
        jnp.sum(to_float(own_block(gate_weight)) * grad_gate_weight, axis=1)
        + jnp.sum(to_float(own_block(up_weight)) * grad_up_weight, axis=1)
    ) / own_block(gain_feedforward)
    gain_one = (
        sum_tensor(jnp.sum(to_float(own_block(query_weight)) * grad_query_weight, axis=1))
        + jnp.sum(to_float(own_block(keyval_weight)) * grad_keyval_weight, axis=1)
    ) / own_block(gain_attention)
    return (
        block_output,
        grad_rows,
        gain_one,
        grad_query_weight,
        grad_keyval_weight,
        grad_output_weight,
        gain_two,
        grad_gate_weight,
        grad_up_weight,
        grad_down,
    )


def solution(mesh):
    placed = (
        P(("dp", "tensor"), None),
        P(("dp", "tensor"), None),
        P(),
        P(),
        P(None, "tensor"),
        P(),
        P(None, "tensor"),
        P(),
        P(None, "tensor"),
        P(None, "tensor"),
        P(None, "tensor"),
    )
    return jax.shard_map(
        per_device,
        mesh=mesh,
        in_specs=placed,
        out_specs=(
            P(("dp", "tensor"), None),
            P(("dp", "tensor"), None),
            P("dp"),
            P("dp", "tensor"),
            P("dp", None),
            P("dp", "tensor"),
            P("dp"),
            P("dp", "tensor"),
            P("dp", "tensor"),
            P("dp", "tensor"),
        ),
        check_vma=False,
    )
```
